128 devices in a mesh: ctx: 32 (over x, z, core), head: 4 (over y).
Axes of the slice: x: 4, y: 4, z: 4, core: 2. Of those that a mesh axis runs over, the one named last changes fastest.
Arguments:
- tokens: bfloat16 [16384, 2560], P('ctx', 'head'), may hold values from -6 to 6
- send_rows: int32 [32, 32, 32], P('ctx'), may hold values from 0 to 511, as said below
- send_counts: int32 [32, 32], replicated, may hold values from 0 to 32, as said below
- stretch_segments: int32 [64], replicated, may hold values from 0 to 12, never falling along the last dimension, each value on 1 to 6 neighbouring positions
- main_proj: bfloat16 [2560, 2, 5120], P(None, None, 'head'), may hold values from -0.125 to 0.125
- state_proj: bfloat16 [2560, 256], replicated, may hold values from -0.125 to 0.125
- step_proj: bfloat16 [2560, 80], P(None, 'head'), may hold values from -0.125 to 0.125
- conv_main: float32 [4, 5120], P(None, 'head'), may hold values from -3 to 3
- conv_state: float32 [4, 256], replicated, may hold values from -3 to 3
- step_bias: float32 [80], P('head'), may hold values from -11 to -3.5
- decay_log: float32 [80], P('head'), may hold values from 0 to 1.39
- skip_gain: float32 [80], P('head'), may hold values from 0.05 to 0.8
- norm_gain: float32 [5120], P('head'), may hold values from 0.5 to 1.5
- out_proj: bfloat16 [5120, 2560], P('head'), may hold values from -0.078125 to 0.078125
Outputs:
- mixed: bfloat16 [16384, 2560], P('ctx', 'head')
The draws below stay inside these ranges and needn't reach their ends.
Inputs may be any that keep to these rules, and one draw needn't show every extreme that they name: Entries 0 to send_counts[s, d] - 1 of send_rows[s, d] name distinct rows of generator s's 512; over all d every row of s is named once; other entries are 0. `send_counts`: every row and every column sums to 512. `stretch_segments`: Non-decreasing; a document spans 1 to 6 blocks.
All inputs are finite; a program needn't handle non-finite values.
Results may differ from the reference program's by a relative error of at most 0.015.
Values may be sent and summed in bfloat16 or wider, within the bound.
No kernel may reach another device: no remote copies, remote signals or barrier semaphores. Data moves between devices by JAX's collectives and lax.ppermute only.
A program may use at most 128 MiB of HBM per device.

```python
import math
import jax
import jax.numpy as jnp
import numpy as np
from jax import lax

D = 2560
HEADS = 80
HEAD_DIM = 64
STATE = 128
KERNEL = 4
STRETCH = 256
DOC_STRETCHES = 6
TOK_DEV = 512
DI = 5120
GENS = 32
CAP = 32
TOKENS = 16384
NCHUNK = 64
HEAD_GROUPS = 4


def source_order(sub_key):
    return jax.random.permutation(sub_key, TOK_DEV).astype(jnp.int32)


def routing_plan(key):
    key_order, key_shift, key_rotate, key_rows = jax.random.split(key, 4)
    base = TOK_DEV // GENS
    half = GENS // 2
    order = jax.random.permutation(key_order, GENS).astype(jnp.int32)
    shifts = jax.random.randint(key_shift, (half,), 0, base + 1).astype(jnp.int32)
    shifts = shifts.at[0].set(base)
    weights = jnp.full((GENS,), base, jnp.int32)
    weights = weights.at[order[:half]].set(base + shifts)
    weights = weights.at[order[half:2 * half]].set(base - shifts)
    rotate = jax.random.permutation(key_rotate, GENS).astype(jnp.int32)
    target = jnp.arange(GENS, dtype=jnp.int32)
    counts = weights[(target[None, :] + rotate[:, None]) % GENS]
    orders = jax.vmap(source_order)(jax.random.split(key_rows, GENS))
    begins = jnp.cumsum(counts, axis=1) - counts
    slot_ids = jnp.arange(CAP, dtype=jnp.int32)
    where_at = jnp.minimum(begins[:, :, None] + slot_ids[None, None, :], TOK_DEV - 1)
    picked = jnp.take_along_axis(orders, where_at.reshape(GENS, GENS * CAP), axis=1).reshape(GENS, GENS, CAP)
    filled = slot_ids[None, None, :] < counts[:, :, None]
    rows_sent = jnp.where(filled, picked, 0).astype(jnp.int32)
    return (rows_sent, counts.astype(jnp.int32))


def head_plan(key, quick_share):
    key = jax.random.fold_in(key, 21)
    key_pick, key_rate, key_reach = jax.random.split(key, 3)
    quick_mask = jax.random.uniform(key_pick, (HEADS,), jnp.float32) < quick_share
    rate_log = jax.random.uniform(key_rate, (HEADS,), jnp.float32) * jnp.log(4.0)
    level = jax.random.uniform(key_reach, (HEADS,), jnp.float32)
    chain_len = DOC_STRETCHES * STRETCH * 1.0
    head_reach = jnp.where(quick_mask, 30.0 + 20.0 * level, chain_len * (1.5 + 1.5 * level))
    bias_value = -jnp.log(head_reach) - rate_log - 0.5
    return (rate_log.astype(jnp.float32), bias_value.astype(jnp.float32))


def draw_send_rows(key, part):
    rows_sent, counts = routing_plan(key)
    return rows_sent


def draw_send_counts(key, part):
    rows_sent, counts = routing_plan(key)
    return counts


def draw_tokens(key, part):
    rows_sent, counts = routing_plan(key)
    key = jax.random.fold_in(key, 13)
    key_scale, key_entry = jax.random.split(key)
    low_scale = 0.6
    high_scale = 1.6
    level = jax.random.uniform(key_scale, (NCHUNK,), jnp.float32)
    stretch_scale = jnp.exp(jnp.log(low_scale) + level * (jnp.log(high_scale) - jnp.log(low_scale)))
    arrive_at = jnp.cumsum(counts, axis=0) - counts
    slot_ids = jnp.arange(CAP, dtype=jnp.int32)
    filled = slot_ids[None, None, :] < counts[:, :, None]
    packed_pos = jnp.arange(GENS, dtype=jnp.int32)[None, :, None] * TOK_DEV + arrive_at[:, :, None] + slot_ids[None, None, :]
    row_ids = jnp.where(filled, rows_sent, TOK_DEV).astype(jnp.int32)
    gen_ids = jnp.broadcast_to(jnp.arange(GENS, dtype=jnp.int32)[:, None, None], (GENS, GENS, CAP))
    position = jnp.zeros((GENS, TOK_DEV), jnp.int32).at[gen_ids.reshape(-1), row_ids.reshape(-1)].set(packed_pos.reshape(-1).astype(jnp.int32), mode='drop')
    row_scale = stretch_scale[(position // STRETCH).reshape(TOKENS)]
    entries = jnp.clip(jax.random.normal(key_entry, (TOKENS, D), jnp.float32), -3.5, 3.5)
    return (entries * row_scale[:, None]).astype(jnp.bfloat16)


def draw_decay_log(key, part):
    quick_share = 0.3
    rate_log, bias_value = head_plan(key, quick_share)
    return rate_log


def draw_step_bias(key, part):
    quick_share = 0.3
    rate_log, bias_value = head_plan(key, quick_share)
    return bias_value


def draw_skip_gain(key, part):
    key = jax.random.fold_in(key, 9)
    top_gain = 0.5
    level = jax.random.uniform(key, (HEADS,), jnp.float32)
    return jnp.exp(jnp.log(0.05) + level * (jnp.log(top_gain) - jnp.log(0.05))).astype(jnp.float32)


def levels(key, extent, pieces, smallest, high):
    loudness = 1.0
    for axis_at, parts in pieces:
        heights = jax.random.uniform(jax.random.fold_in(jax.random.fold_in(key, 6), axis_at), (parts,), jnp.float32, smallest / len(pieces), high / len(pieces))
        loudness = loudness * jnp.repeat(jnp.exp(heights), extent[axis_at] // parts).reshape((-1,) + (1,) * (len(extent) - 1 - axis_at))
    return loudness


def length_profile(number_of, total, bound, skew):
    portions = [(1 << 20) // math.isqrt(rank ** skew) + 1 for rank in range(2, number_of + 1)]
    surplus, given = total - bound - (number_of - 1), [1] * (number_of - 1)
    while surplus > 0:
        free = [i for i in range(number_of - 1) if given[i] < bound]
        mass, left = sum([portions[i] for i in free]), surplus
        for i in free:
            addition = min(bound - given[i], max(1, left * portions[i] // mass), surplus)
            given[i] = given[i] + addition
            surplus = surplus - addition
    return np.array([bound] + given)


def uneven(rng, amount, total, reach, skew):
    if amount == 2:
        one = jax.random.randint(rng, (), max(1, total - reach), min(reach, total - 1) + 1)
        return jnp.stack([one, total - one])
    tallies = jnp.asarray(length_profile(amount, total, reach, skew), jnp.int32)
    twos = (amount - 1) // 2
    giver, receiver = tallies[1:1 + 2 * twos:2], tallies[2:2 + 2 * twos:2]
    room = jnp.minimum(giver - 1, reach - receiver)
    shifted = jax.random.randint(jax.random.fold_in(rng, 1), (twos,), 0, 1 << 20) % (room + 1)
    tallies = tallies.at[1:1 + 2 * twos:2].set(giver - shifted).at[2:2 + 2 * twos:2].set(receiver + shifted)
    return tallies[jax.random.permutation(jax.random.fold_in(rng, 2), amount)]


def centred(rng, dims, width, bound, cuts=(), held_as=jnp.bfloat16):
    values = width * jax.random.normal(rng, dims, jnp.float32)
    if cuts:
        values = values * levels(rng, dims, cuts, -0.22, 0.18)
    return jnp.clip(values, -bound, bound).astype(held_as)


def setup_inputs(seed: int = 0) -> dict:
    splits = jax.random.split(jax.random.key(seed), 15)
    return {
        "tokens": draw_tokens(jax.random.fold_in(splits[14], 71), 0),
        "send_rows": draw_send_rows(jax.random.fold_in(splits[14], 71), 0),
        "send_counts": draw_send_counts(jax.random.fold_in(splits[14], 71), 0),
        "stretch_segments": jnp.searchsorted(jnp.cumsum(uneven(splits[3], (NCHUNK + 4) // 5, NCHUNK, DOC_STRETCHES, 0)), jnp.arange(NCHUNK), side="right").astype(jnp.int32),
        "main_proj": centred(splits[4], (D, 2, DI), D ** -0.5, 0.125, ((2, 4),)),
        "state_proj": centred(splits[5], (D, 2 * STATE), D ** -0.5, 0.125),
        "step_proj": centred(splits[6], (D, HEADS), D ** -0.5, 0.125, ((1, 4),)),
        "conv_main": centred(splits[7], (KERNEL, DI), KERNEL ** -0.5, 3.0, ((1, 4),), jnp.float32),
        "conv_state": centred(splits[8], (KERNEL, 2 * STATE), KERNEL ** -0.5, 3.0, (), jnp.float32),
        "step_bias": draw_step_bias(jax.random.fold_in(splits[14], 71), 0),
        "decay_log": draw_decay_log(jax.random.fold_in(splits[14], 71), 0),
        "skip_gain": draw_skip_gain(jax.random.fold_in(splits[14], 71), 0),
        "norm_gain": jnp.clip(1.0 + 0.1 * jax.random.normal(splits[12], (DI,), jnp.float32), 0.5, 1.5),
        "out_proj": centred(splits[13], (DI, D), DI ** -0.5, 0.078125, ((0, 4),)),
    }


def pack_rows(tokens, send_rows, send_counts):
    arrive_at = jnp.cumsum(send_counts, axis=0) - send_counts
    slot_ids = jnp.arange(CAP, dtype=jnp.int32)
    filled = slot_ids[None, None, :] < send_counts[:, :, None]
    sources = jnp.arange(GENS, dtype=jnp.int32)[:, None, None] * TOK_DEV + send_rows
    targets = jnp.arange(GENS, dtype=jnp.int32)[None, :, None] * TOK_DEV + arrive_at[:, :, None] + slot_ids[None, None, :]
    targets = jnp.where(filled, targets, TOKENS).astype(jnp.int32)
    moved = tokens[sources.reshape(-1)]
    return jnp.zeros((TOKENS, D), tokens.dtype).at[targets.reshape(-1)].set(moved, mode='drop')

def reference(tokens, send_rows, send_counts, stretch_segments, main_proj, state_proj, step_proj, conv_main, conv_state, step_bias, decay_log, skip_gain, norm_gain, out_proj):
    packed = pack_rows(tokens, send_rows, send_counts)
    main_flat = main_proj.reshape(D, 2 * DI)
    conv_taps = jnp.concatenate([conv_main, conv_state], axis=1)
    kernel_len = conv_taps.shape[0]
    rates = jnp.exp(decay_log)
    group_width = DI // HEAD_GROUPS
    previous = jnp.concatenate([stretch_segments[:1], stretch_segments[:-1]])
    carry_on = ((stretch_segments == previous) & (jnp.arange(NCHUNK) > 0)).astype(jnp.float32)
    causal = jnp.arange(STRETCH)[:, None] >= jnp.arange(STRETCH)[None, :]
    blocks_in = packed.reshape(NCHUNK, STRETCH, D)

    def one_block(carry, inputs):
        tail_rows, state_now = carry
        block_rows, carry_flag = inputs
        gate_up = jnp.dot(block_rows, main_flat, preferred_element_type=jnp.float32)
        gate_in = gate_up[:, :DI].astype(jnp.bfloat16)
        value_in = gate_up[:, DI:].astype(jnp.bfloat16)
        state_in = jnp.dot(block_rows, state_proj, preferred_element_type=jnp.float32).astype(jnp.bfloat16)
        step_raw = jnp.dot(block_rows, step_proj, preferred_element_type=jnp.float32)
        channels = jnp.concatenate([value_in, state_in], axis=1)
        earlier_rows = jnp.where(carry_flag > 0, tail_rows, jnp.zeros_like(tail_rows))
        extended = jnp.concatenate([earlier_rows, channels], axis=0)
        conv_sum = jnp.zeros((STRETCH, channels.shape[1]), jnp.float32)
        for tap_index in range(kernel_len):
            conv_sum = conv_sum + extended[tap_index:tap_index + STRETCH].astype(jnp.float32) * conv_taps[tap_index]
        activated = jax.nn.silu(conv_sum).astype(jnp.bfloat16)
        values_in = activated[:, :DI].reshape(STRETCH, HEADS, HEAD_DIM)
        b_rows = activated[:, DI:DI + STATE]
        c_rows = activated[:, DI + STATE:]
        step_size = jax.nn.softplus(step_raw + step_bias)
        cum_decay = jnp.cumsum(-rates * step_size, axis=0)
        scores = jnp.dot(c_rows, b_rows.T, preferred_element_type=jnp.float32)
        gaps = cum_decay.T[:, :, None] - cum_decay.T[:, None, :]
        decays = jnp.exp(jnp.where(causal[None], gaps, -1e+30))
        mixing = (scores[None] * decays * step_size.T[:, None, :]).astype(jnp.bfloat16)
        mixing = lax.optimization_barrier(mixing)
        intra = jnp.einsum('hts,shp->thp', mixing.astype(jnp.float32), values_in.astype(jnp.float32))
        weights = jnp.exp(cum_decay[-1][None, :] - cum_decay) * step_size
        weighted_b = (weights[:, :, None] * b_rows[:, None, :].astype(jnp.float32)).astype(jnp.bfloat16)
        weighted_b = lax.optimization_barrier(weighted_b)
        block_state = jnp.einsum('shn,shp->hnp', weighted_b.astype(jnp.float32), values_in.astype(jnp.float32))
        start_state = state_now * carry_flag
        start_low = lax.optimization_barrier(start_state.astype(jnp.bfloat16))
        inter = jnp.exp(cum_decay)[:, :, None] * jnp.einsum('tn,hnp->thp', c_rows.astype(jnp.float32), start_low.astype(jnp.float32))
        combined = intra + inter + skip_gain[None, :, None] * values_in.astype(jnp.float32)
        next_state = jnp.exp(cum_decay[-1])[:, None, None] * start_state + block_state
        gated = combined.reshape(STRETCH, DI) * jax.nn.silu(gate_in.astype(jnp.float32))
        mean_sq = lax.optimization_barrier(jnp.mean(gated * gated, axis=1, keepdims=True))
        normed = (gated * lax.rsqrt(mean_sq + 1e-05) * norm_gain).astype(jnp.bfloat16)
        mixed_sum = jnp.zeros((STRETCH, D), jnp.float32)
        for group_num in range(HEAD_GROUPS):
            low_col = group_num * group_width
            partial_value = jnp.dot(normed[:, low_col:low_col + group_width], out_proj[low_col:low_col + group_width], preferred_element_type=jnp.float32).astype(jnp.bfloat16)
            mixed_sum = mixed_sum + lax.optimization_barrier(partial_value).astype(jnp.float32)
        return ((channels[STRETCH - kernel_len + 1:], next_state), mixed_sum.astype(jnp.bfloat16))
    start_carry = (jnp.zeros((kernel_len - 1, DI + 2 * STATE), jnp.bfloat16), jnp.zeros((HEADS, STATE, HEAD_DIM), jnp.float32))
    final_carry, outputs = lax.scan(one_block, start_carry, (blocks_in, carry_on))
    return outputs.reshape(TOKENS, D)
```

```python
import jax
import jax.numpy as jnp
from jax import lax
from jax.experimental import pallas as pl
from jax.experimental.pallas import tpu as pltpu
from jax.sharding import PartitionSpec as P

BF = jnp.bfloat16
F32 = jnp.float32
STRETCH = 256
TAIL = 16
TILE = 256
LOG2E = 1.4426950408889634
RING = 4
VMEM = 50 * 1024 * 1024


def dot(a, b):
    return jnp.dot(a, b, preferred_element_type=F32)


def turned(value, steps):
    return lax.ppermute(value, "head", [(i, (i + steps) % RING) for i in range(RING)])


def shifted(value, steps):
    count = lax.axis_size("ctx")
    return lax.ppermute(value, "ctx", [(i, i + steps) for i in range(count - steps)])


def silu(v):
    return v * (1.0 / (1.0 + jnp.exp(-v)))


def split3(x):
    high = x.astype(BF).astype(F32)
    rest = x - high
    mid = rest.astype(BF).astype(F32)
    low = (rest - mid).astype(BF).astype(F32)
    return high, mid, low


def pack3(x):
    high, mid, low = split3(x)
    return (high + pltpu.roll(mid, 32, 1) + pltpu.roll(low, 64, 1)).astype(BF)


def spread(tile, width):
    lane = lax.broadcasted_iota(jnp.int32, (128, width), 0)
    col = lax.broadcasted_iota(jnp.int32, (128, width), 1)
    hit = ((lane & 31) == tile * (width // 64) + (col >> 6)) & (lane < 96)
    return jnp.where(hit, 1.0, 0.0).astype(BF)


def params(n=1):
    return pltpu.CompilerParams(
        dimension_semantics=("arbitrary",) * n, vmem_limit_bytes=VMEM
    )


def cost(flops, bytes_accessed, exps=0):
    return pl.CostEstimate(
        flops=int(flops), bytes_accessed=int(bytes_accessed), transcendentals=int(exps)
    )


def whole(shape):
    return pl.BlockSpec(shape, lambda i, ids: (0,) * len(shape))


def tile_of(i):
    return jnp.maximum(i - 1, 0)


def own_body(ids, x, wsd, wv, osd, ov):
    i = pl.program_id(0)

    @pl.when(i == 0)
    def _():
        osd[...] = dot(x[...], wsd[...])

    @pl.when(i > 0)
    def _():
        ov[...] = dot(x[...], wv[...])


def own_part(ids, x, wsd, wv):
    rows, k = x.shape
    nsd, nv = wsd.shape[1], wv.shape[1] // 2
    past = nv // TILE
    return pl.pallas_call(
        own_body,
        grid_spec=pltpu.PrefetchScalarGridSpec(
            num_scalar_prefetch=1,
            grid=(1 + nv // TILE,),
            in_specs=[
                whole((rows, k)),
                pl.BlockSpec((k, nsd), lambda i, ids: (ids[0], 0)),
                pl.BlockSpec((k, TILE), lambda i, ids: (ids[0], past + tile_of(i))),
            ],
            out_specs=[
                whole((rows, nsd)),
                pl.BlockSpec((rows, TILE), lambda i, ids: (0, tile_of(i))),
            ],
        ),
        out_shape=[
            jax.ShapeDtypeStruct((rows, nsd), F32),
            jax.ShapeDtypeStruct((rows, nv), F32),
        ],
        compiler_params=params(),
        cost_estimate=cost(2 * rows * k * (nsd + nv), 2 * k * (nsd + nv) + 4 * rows * (nsd + nv)),
        name="own_part",
    )(ids, x, wsd, wv)


def next_body(ids, x1, x2, wsd1, wsd2, wv1, wv2, asd, av, osd, ov):
    i = pl.program_id(0)

    @pl.when(i == 0)
    def _():
        osd[...] = asd[...] + dot(x1[...], wsd1[...]) + dot(x2[...], wsd2[...])

    @pl.when(i > 0)
    def _():
        ov[...] = av[...] + dot(x1[...], wv1[...]) + dot(x2[...], wv2[...])


def next_part(ids, x1, x2, wsd, wv, asd, av):
    rows, k = x1.shape
    nsd, nv = wsd.shape[1], wv.shape[1] // 2
    past = nv // TILE
    acc = pl.BlockSpec((rows, TILE), lambda i, ids: (0, tile_of(i)))
    return pl.pallas_call(
        next_body,
        grid_spec=pltpu.PrefetchScalarGridSpec(
            num_scalar_prefetch=1,
            grid=(1 + nv // TILE,),
            in_specs=[
                whole((rows, k)),
                whole((rows, k)),
                pl.BlockSpec((k, nsd), lambda i, ids: (ids[1], 0)),
                pl.BlockSpec((k, nsd), lambda i, ids: (ids[2], 0)),
                pl.BlockSpec((k, TILE), lambda i, ids: (ids[1], past + tile_of(i))),
                pl.BlockSpec((k, TILE), lambda i, ids: (ids[2], past + tile_of(i))),
                whole((rows, nsd)),
                acc,
            ],
            out_specs=[whole((rows, nsd)), acc],
        ),
        out_shape=[
            jax.ShapeDtypeStruct((rows, nsd), F32),
            jax.ShapeDtypeStruct((rows, nv), F32),
        ],
        compiler_params=params(),
        cost_estimate=cost(4 * rows * k * (nsd + nv), 4 * k * (nsd + nv) + 8 * rows * (nsd + nv)),
        name="next_part",
    )(ids, x1, x2, wsd, wsd, wv, wv, asd, av)


def conv_block(xs, taps, block, width):
    low = TAIL + block * STRETCH
    total = None
    for k in range(4):
        start = low - 3 + k
        term = xs[start : start + STRETCH, :width] * taps[k : k + 1, :]
        total = term if total is None else total + term
    return silu(total).astype(BF)


def convolved(ids, xs, taps, width, put):
    @pl.when(ids[4] == 0)
    def _():
        xs[TAIL - 8 : TAIL, :] = jnp.zeros((8, xs.shape[1]), F32)

    put(0, conv_block(xs, taps, 0, width))

    @pl.when(ids[5] == 0)
    def _():
        xs[TAIL + STRETCH - 8 : TAIL + STRETCH, :] = jnp.zeros((8, xs.shape[1]), F32)

    put(1, conv_block(xs, taps, 1, width))


def state_body(
    ids, x1, x2, wsd, wv, asd, av, taps_s, taps_v, heads,
    act, bc, cum3, cum_t, step_t, ecum3, state0, state_dev, rows_out, payload,
    xs, bt, w3, last3,
):
    i = pl.program_id(0)
    n1 = x1.shape[0]

    @pl.when(i == 0)
    def _():
        first = asd[:n1, :] + dot(x1[...], wsd[...])
        second = asd[n1:, :] + dot(x2[...], wsd[...])
        xs[:n1, :] = first[:, :256].astype(BF).astype(F32)
        xs[n1:, :] = second[:, :256].astype(BF).astype(F32)

        def put(block, value):
            bc[block * STRETCH : (block + 1) * STRETCH, :] = value
            bt[block] = jnp.transpose(value[:, :128].astype(F32)).astype(BF)

        convolved(ids, xs, taps_s, 256, put)
        raws = (first[TAIL:, 256:], second[:, 256:])
        lane = lax.broadcasted_iota(jnp.int32, (STRETCH, 128), 1)
        row_id = lax.broadcasted_iota(jnp.int32, (STRETCH, STRETCH), 0)
        col_id = lax.broadcasted_iota(jnp.int32, (STRETCH, STRETCH), 1)
        below = jnp.where(row_id >= col_id, 1.0, 0.0).astype(BF)
        lasts = []
        for block in range(2):
            rows = slice(block * STRETCH, (block + 1) * STRETCH)
            raw = raws[block] + heads[0:1, :]
            small = jnp.exp(-jnp.abs(raw))
            one = 1.0 + small
            log_one = jnp.where(one == 1.0, small, jnp.log(one) * (small / (one - 1.0 + 1e-30)))
            step = jnp.where(lane < 32, jnp.maximum(raw, 0.0) + log_one, 0.0)
            decay = pack3(step * (heads[1:2, :] * (-LOG2E)))
            sums = dot(below, decay)
            sums = sums + pltpu.roll(sums, 96, 1) + pltpu.roll(sums, 64, 1)
            sums = jnp.where(lane < 32, sums, 0.0)
            final = sums[STRETCH - 1 : STRETCH, :]
            cum3[rows, :] = pack3(sums)
            cum_t[block] = jnp.transpose(sums)[:32]
            step_t[block] = jnp.transpose(step)[:32]
            keep = jnp.where(lane < 32, jnp.exp2(sums), 0.0)
            ecum3[rows, :] = pack3(keep)
            w3[rows, :] = pack3(jnp.exp2(final - sums) * step)
            lasts.append(jnp.where(lane[:1] < 32, jnp.exp2(final), 0.0))
        pad_row = lax.broadcasted_iota(jnp.int32, (16, 128), 0)
        last3[...] = pack3(
            jnp.where(pad_row == 0, lasts[0], jnp.where(pad_row == 1, lasts[1], 0.0))
        )

    @pl.when(i > 0)
    def _():
        xs[:n1, :] = (av[:n1, :] + dot(x1[...], wv[...])).astype(BF).astype(F32)
        xs[n1:, :] = (av[n1:, :] + dot(x2[...], wv[...])).astype(BF).astype(F32)
        select = spread(i - 1, TILE)
        states = []

        def put(block, value):
            rows = slice(block * STRETCH, (block + 1) * STRETCH)
            act[rows, :] = value
            weighted = (value.astype(F32) * dot(w3[rows, :], select)).astype(BF)
            states.append(dot(bt[block], weighted))

        convolved(ids, xs, taps_v, TILE, put)
        ends = dot(last3[...], select)
        carry0 = jnp.where(ids[4] > 0, 1.0, 0.0)
        carry1 = jnp.where(ids[5] > 0, 1.0, 0.0)
        end0, end1 = ends[0:1, :], ends[1:2, :] * carry1
        whole_decay = end0 * carry0 * end1
        device = states[1] + end1 * states[0]
        state0[...] = states[0]
        state_dev[...] = device
        row = lax.broadcasted_iota(jnp.int32, (16, TILE), 0)
        rows_out[...] = jnp.where(row[:8] == 0, end0, jnp.where(row[:8] == 1, whole_decay, 0.0))
        high, mid, low = split3(whole_decay)
        payload[:128, :] = device.astype(BF)
        payload[128:, :] = jnp.where(
            row == 0, high, jnp.where(row == 1, mid, jnp.where(row == 2, low, 0.0))
        ).astype(BF)


def state_part(ids, x1, x2, wsd, wv, asd, av, taps_s, taps_v, heads):
    k = x1.shape[1]
    n1, n2 = x1.shape[0], x2.shape[0]
    rows = n1 + n2
    tok = rows - TAIL
    nsd, nv = wsd.shape[1], wv.shape[1] // 2
    past = nv // TILE

    def tiled(height):
        return pl.BlockSpec((height, TILE), lambda i, ids: (0, tile_of(i)))

    return pl.pallas_call(
        state_body,
        grid_spec=pltpu.PrefetchScalarGridSpec(
            num_scalar_prefetch=1,
            grid=(1 + nv // TILE,),
            in_specs=[
                whole((n1, k)),
                whole((n2, k)),
                pl.BlockSpec((k, nsd), lambda i, ids: (ids[3], 0)),
                pl.BlockSpec((k, TILE), lambda i, ids: (ids[3], past + tile_of(i))),
                whole((rows, nsd)),
                tiled(rows),
                whole((4, 256)),
                tiled(4),
                whole((8, 128)),
            ],
            out_specs=[
                tiled(tok),
                whole((tok, 256)),
                whole((tok, 128)),
                whole((2, 32, STRETCH)),
                whole((2, 32, STRETCH)),
                whole((tok, 128)),
                tiled(128),
                tiled(128),
                tiled(8),
                tiled(144),
            ],
            scratch_shapes=[
                pltpu.VMEM((rows, TILE), F32),
                pltpu.VMEM((2, 128, STRETCH), BF),
                pltpu.VMEM((tok, 128), BF),
                pltpu.VMEM((16, 128), BF),
            ],
        ),
        out_shape=[
            jax.ShapeDtypeStruct((tok, nv), BF),
            jax.ShapeDtypeStruct((tok, 256), BF),
            jax.ShapeDtypeStruct((tok, 128), BF),
            jax.ShapeDtypeStruct((2, 32, STRETCH), F32),
            jax.ShapeDtypeStruct((2, 32, STRETCH), F32),
            jax.ShapeDtypeStruct((tok, 128), BF),
            jax.ShapeDtypeStruct((128, nv), F32),
            jax.ShapeDtypeStruct((128, nv), F32),
            jax.ShapeDtypeStruct((8, nv), F32),
            jax.ShapeDtypeStruct((144, nv), BF),
        ],
        compiler_params=params(),
        cost_estimate=cost(2 * rows * k * (nsd + nv), 2 * k * (nsd + nv) + 8 * rows * (nsd + nv)),
        name="state_part",
    )(ids, x1, x2, wsd, wv, asd, av, taps_s, taps_v, heads)


def join_body(state, row, got, out):
    out[...] = (state[...] + row[1:2, :] * got[:128, :].astype(F32)).astype(BF)


def join_part(state, row, got):
    return pl.pallas_call(
        join_body,
        out_shape=jax.ShapeDtypeStruct(state.shape, BF),
        compiler_params=pltpu.CompilerParams(vmem_limit_bytes=VMEM),
        cost_estimate=cost(2 * state.size, 8 * state.size),
        name="join_part",
    )(state, row, got)


def mix_body(ids, x, r, l, o1, o2, wg, act, bc, cum3, cum_t, step_t, ecum3, skip, p_out, q_out, sc):
    i = pl.program_id(0)
    k = x.shape[1]

    @pl.when(i == 0)
    def _():
        row_id = lax.broadcasted_iota(jnp.int32, (STRETCH, STRETCH), 0)
        col_id = lax.broadcasted_iota(jnp.int32, (STRETCH, STRETCH), 1)
        for block in range(2):
            rows = slice(block * STRETCH, (block + 1) * STRETCH)
            scores = lax.dot_general(
                bc[rows, 128:], bc[rows, :128], (((1,), (1,)), ((), ())), preferred_element_type=F32
            )
            sc[block] = jnp.where(row_id >= col_id, scores, 0.0)

    def weights(at):
        return wg[pl.ds(pl.multiple_of(ids[at] * k, 128), k), :]

    select = spread(i, TILE)
    lane = lax.broadcasted_iota(jnp.int32, (128, STRETCH), 0)
    group = lax.broadcasted_iota(jnp.int32, (STRETCH, TILE), 1) >> 6
    half = STRETCH // 2
    for block in range(2):
        rows = slice(block * STRETCH, (block + 1) * STRETCH)
        here = slice(TAIL + block * STRETCH, TAIL + (block + 1) * STRETCH)
        other = o1[TAIL:, :] if block == 0 else o2[...]
        gate = (
            dot(x[here, :], weights(0))
            + dot(r[here, :], weights(1))
            + dot(l[here, :], weights(2))
            + dot(other, weights(3))
        )
        gate = silu(gate.astype(BF).astype(F32))
        values = act[rows, :]
        top = jnp.zeros((half, TILE), F32)
        bottom = jnp.zeros((half, TILE), F32)
        for j in range(TILE // 64):
            h = i * (TILE // 64) + j
            pick = jnp.where(((lane & 31) == h) & (lane < 96), 1.0, 0.0).astype(BF)
            cum = dot(cum3[rows, :], pick)
            cum_s = cum_t[block, pl.ds(h, 1), :]
            step_s = step_t[block, pl.ds(h, 1), :]
            mine = jnp.where(group == j, values, jnp.zeros_like(values))
            m_top = (
                sc[block, :half, :half]
                * jnp.exp2(jnp.minimum(cum[:half, :half] - cum_s[:, :half], 0.0))
                * step_s[:, :half]
            ).astype(BF)
            m_bottom = (
                sc[block, half:, :]
                * jnp.exp2(jnp.minimum(cum[half:, :] - cum_s, 0.0))
                * step_s
            ).astype(BF)
            top = top + dot(m_top, mine[:half, :])
            bottom = bottom + dot(m_bottom, mine)
        within = jnp.concatenate([top, bottom], axis=0)
        p_out[rows, :] = (within + skip[0:1, :] * values.astype(F32)) * gate
        q_out[rows, :] = dot(ecum3[rows, :], select) * gate


def mix_part(ids, x, r, l, o1, o2, wg, act, bc, cum3, cum_t, step_t, ecum3, skip):
    tok, nv = act.shape

    def tiled(height):
        return pl.BlockSpec((height, TILE), lambda i, ids: (0, i))

    return pl.pallas_call(
        mix_body,
        grid_spec=pltpu.PrefetchScalarGridSpec(
            num_scalar_prefetch=1,
            grid=(nv // TILE,),
            in_specs=[
                whole(x.shape),
                whole(r.shape),
                whole(l.shape),
                whole(o1.shape),
                whole(o2.shape),
                tiled(wg.shape[0]),
                tiled(tok),
                whole(bc.shape),
                whole(cum3.shape),
                whole(cum_t.shape),
                whole(step_t.shape),
                whole(ecum3.shape),
                tiled(8),
            ],
            out_specs=[tiled(tok), tiled(tok)],
            scratch_shapes=[pltpu.VMEM((2, STRETCH, STRETCH), F32)],
        ),
        out_shape=[jax.ShapeDtypeStruct((tok, nv), F32)] * 2,
        compiler_params=params(),
        cost_estimate=cost(tok * wg.size, wg.size + 10 * tok * nv, 20 * tok * 256),
        name="mix_part",
    )(ids, x, r, l, o1, o2, wg, act, bc, cum3, cum_t, step_t, ecum3, skip)


def gated_body(ids, p, q, bc, got1, got2, state0, rows_in, gain, wo, z, far, squares, acc, sq):
    i = pl.program_id(0)
    carry0 = jnp.where(ids[4] > 0, 1.0, 0.0)
    carry1 = jnp.where(ids[5] > 0, 1.0, 0.0)
    tail = got1[128:, :].astype(F32)
    decay = tail[0:1, :] + tail[1:2, :] + tail[2:3, :]
    entering = got1[:128, :].astype(F32) + decay * got2[...].astype(F32)
    start0 = entering * carry0
    start1 = (rows_in[0:1, :] * start0 + state0[...]) * carry1
    sums = []
    for block, start in ((0, start0), (1, start1)):
        rows = slice(block * STRETCH, (block + 1) * STRETCH)
        from_start = dot(bc[rows, 128:], start.astype(BF))
        gated = p[rows, :] + q[rows, :] * from_start
        square = gated * gated
        sums.append(square[:, :128] + square[:, 128:])
        z[rows, :] = (gated * gain[0:1, :]).astype(BF)
    part = dot(z[...], wo[...])
    square = jnp.concatenate(sums, axis=0)

    @pl.when(i == 0)
    def _():
        acc[...] = part
        sq[...] = square

    @pl.when(i > 0)
    def _():
        acc[...] += part
        sq[...] += square

    @pl.when(i == pl.num_programs(0) - 1)
    def _():
        far[...] = acc[...].astype(BF)
        flat = jnp.sum(jnp.transpose(sq[...]), axis=0, keepdims=True)
        squares[...] = jnp.broadcast_to(flat, squares.shape)


def gated_part(ids, p, q, bc, got1, got2, state0, rows_in, gain, wo):
    tok, nv = p.shape
    ncol = wo.shape[1] // RING

    def tiled(height):
        return pl.BlockSpec((height, TILE), lambda i, ids: (0, i))

    return pl.pallas_call(
        gated_body,
        grid_spec=pltpu.PrefetchScalarGridSpec(
            num_scalar_prefetch=1,
            grid=(nv // TILE,),
            in_specs=[
                tiled(tok),
                tiled(tok),
                whole(bc.shape),
                tiled(144),
                tiled(128),
                tiled(128),
                tiled(8),
                tiled(8),
                pl.BlockSpec((TILE, ncol), lambda i, ids: (i, ids[3])),
            ],
            out_specs=[tiled(tok), whole((tok, ncol)), whole((8, tok))],
            scratch_shapes=[pltpu.VMEM((tok, ncol), F32), pltpu.VMEM((tok, 128), F32)],
        ),
        out_shape=[
            jax.ShapeDtypeStruct((tok, nv), BF),
            jax.ShapeDtypeStruct((tok, ncol), BF),
            jax.ShapeDtypeStruct((8, tok), F32),
        ],
        compiler_params=params(),
        cost_estimate=cost(2 * tok * nv * (ncol + 128), 10 * tok * nv + 2 * nv * ncol),
        name="gated_part",
    )(ids, p, q, bc, got1, got2, state0, rows_in, gain, wo)


def near_body(ids, z, wo, out):
    out[0] = dot(z[...], wo[...]).astype(BF)


def near_part(ids, z, wo, ats, name):
    tok, nv = z.shape
    ncol = wo.shape[1] // RING
    first = ats[0]
    step = ats[1] - ats[0] if len(ats) > 1 else 0
    return pl.pallas_call(
        near_body,
        grid_spec=pltpu.PrefetchScalarGridSpec(
            num_scalar_prefetch=1,
            grid=(len(ats),),
            in_specs=[
                whole((tok, nv)),
                pl.BlockSpec((nv, ncol), lambda i, ids: (0, ids[first + step * i])),
            ],
            out_specs=pl.BlockSpec((1, tok, ncol), lambda i, ids: (i, 0, 0)),
        ),
        out_shape=jax.ShapeDtypeStruct((len(ats), tok, ncol), BF),
        compiler_params=params(),
        cost_estimate=cost(2 * tok * nv * ncol * len(ats), 2 * nv * ncol * len(ats) + 4 * tok * nv),
        name=name,
    )(ids, z, wo)


def add_body(a1, b1, a2, b2, o1, o2):
    o1[...] = (a1[...].astype(F32) + b1[...].astype(F32)).astype(BF)
    o2[...] = (a2[...].astype(F32) + b2[...].astype(F32)).astype(BF)


def add_part(a1, b1, a2, b2):
    shape = jax.ShapeDtypeStruct(a1.shape, BF)
    return pl.pallas_call(
        add_body,
        out_shape=[shape, shape],
        compiler_params=pltpu.CompilerParams(vmem_limit_bytes=VMEM),
        cost_estimate=cost(2 * a1.size, 12 * a1.size),
        name="add_part",
    )(a1, b1, a2, b2)


def final_body(own, top_r, low_r, top_l, low_l, s0, s1, s2, s3, out):
    total = s0[...] + s1[...] + s2[...] + s3[...]
    inv = lax.rsqrt(total * (1.0 / 5120.0) + 1e-05)
    inv = jnp.transpose(jnp.broadcast_to(inv[0:1, :], (128, inv.shape[1])))
    half = STRETCH
    for low, r, l in ((0, top_r, top_l), (half, low_r, low_l)):
        value = (
            own[0, low : low + half, :].astype(F32) + r[...].astype(F32) + l[...].astype(F32)
        )
        scale = inv[low : low + half, :]
        for c in range(0, value.shape[1], 128):
            out[low : low + half, c : c + 128] = (value[:, c : c + 128] * scale).astype(BF)


def final_part(own, top_r, low_r, top_l, low_l, squares):
    shape = own.shape[1:]
    return pl.pallas_call(
        final_body,
        out_shape=jax.ShapeDtypeStruct(shape, BF),
        compiler_params=pltpu.CompilerParams(vmem_limit_bytes=VMEM),
        cost_estimate=cost(4 * own.size, 8 * own.size),
        name="final_part",
    )(own, top_r, low_r, top_l, low_l, *squares)


def on_device(
    tokens,
    send_rows,
    send_counts,
    stretch_segments,
    main_proj,
    state_proj,
    step_proj,
    conv_main,
    conv_state,
    step_bias,
    decay_log,
    skip_gain,
    norm_gain,
    out_proj,
):
    ctx = lax.axis_index("ctx").astype(jnp.int32)
    head = lax.axis_index("head").astype(jnp.int32)
    tok, width = tokens.shape
    sources, slots = send_rows.shape[1:]
    heads = step_bias.shape[0]
    inner = main_proj.shape[2]
    head_dim = inner // heads

    send_list = send_rows.reshape(sources * slots)
    pick = (send_list[:, None] == jnp.arange(tok, dtype=jnp.int32)[None, :]).astype(BF)
    outgoing = dot(pick, tokens).astype(BF).reshape(sources, slots, width)
    arrived = lax.all_to_all(outgoing, "ctx", split_axis=0, concat_axis=0, tiled=True)

    blocks = tok // STRETCH
    block_ids = ctx * blocks + jnp.arange(blocks, dtype=jnp.int32)
    segment = jnp.take(stretch_segments, block_ids)
    before = jnp.take(stretch_segments, jnp.maximum(block_ids - 1, 0))
    carry = ((segment == before) & (block_ids > 0)).astype(jnp.int32)
    ring = jnp.stack([head, head + 3, head + 1, head + 2]) % RING
    ids = jnp.concatenate([ring, carry]).astype(jnp.int32)
    wm = main_proj.reshape(main_proj.shape[0], 2 * inner)
    wsd = jnp.concatenate(
        [state_proj, jnp.pad(step_proj, ((0, 0), (0, 128 - heads)))], axis=1
    )
    head_rows = jnp.zeros((8, 128), F32)
    head_rows = head_rows.at[0, :heads].set(step_bias).at[1, :heads].set(jnp.exp(decay_log))
    skip = jnp.broadcast_to(jnp.repeat(skip_gain, head_dim)[None, :], (8, inner))
    gain = jnp.broadcast_to(norm_gain[None, :], (8, inner))

    column = jnp.take(send_counts, ctx, axis=1)
    ends = jnp.cumsum(column)
    begins = ends - column
    position = jnp.arange(tok, dtype=jnp.int32)
    slot = position[:, None] - begins[None, :]
    inside = (slot >= 0) & (slot < column[None, :])
    flat = jnp.sum(
        jnp.where(inside, slot + jnp.arange(sources, dtype=jnp.int32)[None, :] * slots, 0), axis=1
    )
    place = (flat[:, None] == jnp.arange(sources * slots, dtype=jnp.int32)[None, :]).astype(BF)
    arrived, wm, wsd, place = lax.optimization_barrier((arrived, wm, wsd, place))
    packed = dot(place, arrived.reshape(sources * slots, width)).astype(BF)
    tail = shifted(packed[tok - TAIL :], 1)
    x = jnp.concatenate([tail, packed], axis=0)

    cut = TAIL + STRETCH
    r = turned(x, 1)
    l = turned(x, -1)
    acc_sd, acc_v = own_part(ids, x, wsd, wm)
    r, l, acc_sd, acc_v = lax.optimization_barrier((r, l, acc_sd, acc_v))
    o1 = turned(r[:cut], 1)
    o2 = turned(l[cut:], -1)
    acc_sd, acc_v = next_part(ids, r, l, wsd, wm, acc_sd, acc_v)
    o1, o2, acc_sd, acc_v = lax.optimization_barrier((o1, o2, acc_sd, acc_v))
    act, bc, cum3, cum_t, step_t, ecum3, state0, state_dev, rows_out, payload = state_part(
        ids, o1, o2, wsd, wm, acc_sd, acc_v, conv_state, conv_main, head_rows
    )

    got1 = shifted(payload, 1)
    joined = join_part(state_dev, rows_out, got1)
    got2 = shifted(joined, 2)
    p, q = mix_part(ids, x, r, l, o1, o2, wm, act, bc, cum3, cum_t, step_t, ecum3, skip)

    z, far, squares = gated_part(
        ids, p, q, bc, got1, got2, state0, rows_out, gain, out_proj
    )
    half = STRETCH
    far_r = turned(far[:half], 1)
    far_l = turned(far[half:], -1)
    near = near_part(ids, z, out_proj, (1, 2), "near_part")
    low_r = turned(near[1, half:], 1)
    top_l = turned(near[0, :half], -1)
    sq_r = turned(squares, 1)
    sq_l = turned(squares, -1)
    sq_o = turned(squares, 2)
    own = near_part(ids, z, out_proj, (0,), "mine_part")
    sum_r, sum_l = add_part(near[1, :half], far_r, near[0, half:], far_l)
    top_r = turned(sum_r, 1)
    low_l = turned(sum_l, -1)
    return final_part(own, top_r, low_r, top_l, low_l, (squares, sq_r, sq_l, sq_o))


def solution(mesh):
    return jax.shard_map(
        on_device,
        mesh=mesh,
        in_specs=(
            P("ctx", "head"),
            P("ctx", None, None),
            P(),
            P(),
            P(None, None, "head"),
            P(),
            P(None, "head"),
            P(None, "head"),
            P(),
            P("head"),
            P("head"),
            P("head"),
            P("head"),
            P("head", None),
        ),
        out_specs=P("ctx", "head"),
        check_vma=False,
    )
```

```python
import jax
import jax.numpy as jnp
from jax import lax
from jax.experimental import pallas as pl
from jax.experimental.pallas import tpu as pltpu
from jax.sharding import PartitionSpec as P

BF = jnp.bfloat16
F32 = jnp.float32
STRETCH = 256
TAIL = 16
TILE = 256
LOG2E = 1.4426950408889634
RING = 4
VMEM = 16 * 1024 * 1024


def dot(a, b):
    return jnp.dot(a, b, preferred_element_type=F32)


def turned(value, steps):
    return lax.ppermute(value, "head", [(i, (i + steps) % RING) for i in range(RING)])


def shifted(value, steps):
    count = lax.axis_size("ctx")
    return lax.ppermute(value, "ctx", [(i, i + steps) for i in range(count - steps)])


def silu(v):
    return v * (1.0 / (1.0 + jnp.exp(-v)))


def split3(x):
    high = x.astype(BF).astype(F32)
    rest = x - high
    mid = rest.astype(BF).astype(F32)
    low = (rest - mid).astype(BF).astype(F32)
    return high, mid, low


def pack3(x):
    high, mid, low = split3(x)
    return (high + pltpu.roll(mid, 32, 1) + pltpu.roll(low, 64, 1)).astype(BF)


def spread(tile, width):
    lane = lax.broadcasted_iota(jnp.int32, (128, width), 0)
    col = lax.broadcasted_iota(jnp.int32, (128, width), 1)
    hit = ((lane & 31) == tile * (width // 64) + (col >> 6)) & (lane < 96)
    return jnp.where(hit, 1.0, 0.0).astype(BF)


def call(body, outs, args, name, flops, exps=0, scratch=()):
    size = sum(a.size * a.dtype.itemsize for a in args[1:]) + sum(
        o.size * o.dtype.itemsize for o in outs
    )
    return pl.pallas_call(
        body,
        in_specs=[pl.BlockSpec(memory_space=pltpu.SMEM)]
        + [pl.BlockSpec(memory_space=pltpu.VMEM)] * (len(args) - 1),
        out_specs=[pl.BlockSpec(memory_space=pltpu.VMEM)] * len(outs),
        out_shape=outs,
        scratch_shapes=scratch,
        compiler_params=pltpu.CompilerParams(vmem_limit_bytes=VMEM),
        cost_estimate=pl.CostEstimate(
            flops=int(flops), bytes_accessed=int(size), transcendentals=int(exps)
        ),
        name=name,
    )(*args)


def shape(dims, dtype=F32):
    return jax.ShapeDtypeStruct(dims, dtype)


def chunk_of(ids, at, k):
    return pl.ds(pl.multiple_of(ids[at] * k, 128), k)


def wide(j):
    return slice(j * TILE, (j + 1) * TILE)


def block_rows(block):
    return slice(block * STRETCH, (block + 1) * STRETCH)


def own_body(ids, x, wsd, wm, acc):
    at = chunk_of(ids, 0, x.shape[1])
    acc[:, 2560:] = dot(x[...], wsd[at, :])
    for j in range(10):
        acc[:, wide(j)] = dot(x[...], wm[at, wide(j)])


def own_part(ids, x, wsd, wm):
    rows, k = x.shape
    n = wsd.shape[1] + wm.shape[1]
    return call(own_body, [shape((rows, n))], (ids, x, wsd, wm), "own_part", 2 * rows * k * n)[0]


def next_body(ids, r, l, wsd, wm, before, acc):
    k = r.shape[1]
    at_r, at_l = chunk_of(ids, 1, k), chunk_of(ids, 2, k)
    acc[:, 2560:] = before[:, 2560:] + dot(r[...], wsd[at_r, :]) + dot(l[...], wsd[at_l, :])
    for j in range(10):
        c = wide(j)
        acc[:, c] = before[:, c] + dot(r[...], wm[at_r, c]) + dot(l[...], wm[at_l, c])


def next_part(ids, r, l, wsd, wm, acc):
    rows, k = r.shape
    n = acc.shape[1]
    return call(
        next_body, [shape((rows, n))], (ids, r, l, wsd, wm, acc), "next_part", 4 * rows * k * n
    )[0]


def tail_body(ids, t, t_r, t_l, t_o, wsd, wm, out):
    k = t.shape[1]
    total_s = jnp.zeros((TAIL, 256), F32)
    totals = [jnp.zeros((TAIL, TILE), F32)] * 5
    for at, piece in enumerate((t, t_r, t_l, t_o)):
        place = chunk_of(ids, at, k)
        total_s = total_s + dot(piece[...], wsd[place, :256])
        for j in range(5):
            totals[j] = totals[j] + dot(piece[...], wm[place, wide(5 + j)])
    keep = ids[4] > 0
    for j in range(5):
        out[:, wide(j)] = jnp.where(keep, totals[j].astype(BF).astype(F32), 0.0)
    out[:, 1280:] = jnp.where(keep, total_s.astype(BF).astype(F32), 0.0)


def tail_part(ids, t, t_r, t_l, t_o, wsd, wm):
    return call(
        tail_body,
        [shape((TAIL, 1536))],
        (ids, t, t_r, t_l, t_o, wsd, wm),
        "tail_part",
        2 * 256 * 2560 * 1536,
    )[0]


SEG = STRETCH + 8


def convolved(ids, xs, first, second, before, taps):
    xs[:8, :] = before
    xs[8:SEG, :] = first
    xs[SEG : SEG + 8, :] = jnp.where(ids[5] > 0, first[STRETCH - 8 :, :], 0.0)
    xs[SEG + 8 :, :] = second
    result = []
    for block in range(2):
        total = None
        for k in range(4):
            low = block * SEG + 5 + k
            term = xs[low : low + STRETCH, :] * taps[k : k + 1, :]
            total = term if total is None else total + term
        result.append(silu(total).astype(BF))
    return result


def rounded(x):
    return x.astype(BF).astype(F32)


def state_body(
    ids, o1, o2, wsd, wm, acc, tail, taps_s, taps_v, heads,
    act, bc, cum3, cum_t, step_t, ecum3, state0, state_dev, rows_out, payload,
    xs, bt, w3, last3,
):
    k = o1.shape[1]
    at = chunk_of(ids, 3, k)
    first = acc[:STRETCH, 2560:] + dot(o1[...], wsd[at, :])
    second = acc[STRETCH:, 2560:] + dot(o2[...], wsd[at, :])
    pair = convolved(
        ids, xs.at[0], rounded(first[:, :256]), rounded(second[:, :256]), tail[8:, 1280:], taps_s
    )
    lane = lax.broadcasted_iota(jnp.int32, (STRETCH, 128), 1)
    row_id = lax.broadcasted_iota(jnp.int32, (STRETCH, STRETCH), 0)
    col_id = lax.broadcasted_iota(jnp.int32, (STRETCH, STRETCH), 1)
    below = jnp.where(row_id >= col_id, 1.0, 0.0).astype(BF)
    lasts = []
    for block, raw in ((0, first[:, 256:]), (1, second[:, 256:])):
        rows = block_rows(block)
        bc[rows, :] = pair[block]
        bt[block] = jnp.transpose(pair[block][:, :128].astype(F32)).astype(BF)
        raw = raw + heads[0:1, :]
        small = jnp.exp(-jnp.abs(raw))
        one = 1.0 + small
        log_one = jnp.where(one == 1.0, small, jnp.log(one) * (small / (one - 1.0 + 1e-30)))
        step = jnp.where(lane < 32, jnp.maximum(raw, 0.0) + log_one, 0.0)
        decay = pack3(step * (heads[1:2, :] * (-LOG2E)))
        sums = dot(below, decay)
        sums = sums + pltpu.roll(sums, 96, 1) + pltpu.roll(sums, 64, 1)
        sums = jnp.where(lane < 32, sums, 0.0)
        final = sums[STRETCH - 1 : STRETCH, :]
        cum3[rows, :] = pack3(sums)
        cum_t[block] = jnp.transpose(sums)[:32]
        step_t[block] = jnp.transpose(step)[:32]
        ecum3[rows, :] = pack3(jnp.where(lane < 32, jnp.exp2(sums), 0.0))
        w3[rows, :] = pack3(jnp.exp2(final - sums) * step)
        lasts.append(jnp.where(lane[:1] < 32, jnp.exp2(final), 0.0))
    pad_row = lax.broadcasted_iota(jnp.int32, (16, 128), 0)
    last3[...] = pack3(jnp.where(pad_row == 0, lasts[0], jnp.where(pad_row == 1, lasts[1], 0.0)))
    carry0 = jnp.where(ids[4] > 0, 1.0, 0.0)
    carry1 = jnp.where(ids[5] > 0, 1.0, 0.0)
    row = lax.broadcasted_iota(jnp.int32, (16, TILE), 0)
    for j in range(5):
        c = wide(j)
        a = wide(5 + j)
        first = rounded(acc[:STRETCH, a] + dot(o1[...], wm[at, a]))
        second = rounded(acc[STRETCH:, a] + dot(o2[...], wm[at, a]))
        pair = convolved(ids, xs.at[1 + j % 2], first, second, tail[8:, c], taps_v[:, c])
        select = spread(j, TILE)
        states = []
        for block in range(2):
            rows = block_rows(block)
            act[rows, c] = pair[block]
            weighted = (pair[block].astype(F32) * dot(w3[rows, :], select)).astype(BF)
            states.append(dot(bt[block], weighted))
        ends = dot(last3[...], select)
        end0, end1 = ends[0:1, :], ends[1:2, :] * carry1
        whole_decay = end0 * carry0 * end1
        device = states[1] + end1 * states[0]
        state0[:, c] = states[0]
        state_dev[:, c] = device
        rows_out[:, c] = jnp.where(row[:8] == 0, end0, jnp.where(row[:8] == 1, whole_decay, 0.0))
        high, mid, low = split3(whole_decay)
        payload[:128, c] = device.astype(BF)
        payload[128:, c] = jnp.where(
            row == 0, high, jnp.where(row == 1, mid, jnp.where(row == 2, low, 0.0))
        ).astype(BF)


def state_part(ids, o1, o2, wsd, wm, acc, tail, taps_s, taps_v, heads):
    tok = acc.shape[0]
    return call(
        state_body,
        [
            shape((tok, 1280), BF),
            shape((tok, 256), BF),
            shape((tok, 128), BF),
            shape((2, 32, STRETCH)),
            shape((2, 32, STRETCH)),
            shape((tok, 128), BF),
            shape((128, 1280)),
            shape((128, 1280)),
            shape((8, 1280)),
            shape((144, 1280), BF),
        ],
        (ids, o1, o2, wsd, wm, acc, tail, taps_s, taps_v, heads),
        "state_part",
        2 * tok * 640 * 1664 * 2,
        scratch=[
            pltpu.VMEM((3, 2 * SEG, TILE), F32),
            pltpu.VMEM((2, 128, STRETCH), BF),
            pltpu.VMEM((tok, 128), BF),
            pltpu.VMEM((16, 128), BF),
        ],
    )


def join_body(ids, state, row, got, out):
    out[...] = (state[...] + row[1:2, :] * got[:128, :].astype(F32)).astype(BF)


def join_part(ids, state, row, got):
    return call(
        join_body, [shape(state.shape, BF)], (ids, state, row, got), "join_part", 2 * state.size
    )[0]


def mix_body(ids, o1, o2, wm, acc, act, bc, cum3, cum_t, step_t, ecum3, skip, p_out, q_out, sc):
    k = o1.shape[1]
    at = chunk_of(ids, 3, k)
    row_id = lax.broadcasted_iota(jnp.int32, (STRETCH, STRETCH), 0)
    col_id = lax.broadcasted_iota(jnp.int32, (STRETCH, STRETCH), 1)
    for block in range(2):
        rows = block_rows(block)
        scores = lax.dot_general(
            bc[rows, 128:], bc[rows, :128], (((1,), (1,)), ((), ())), preferred_element_type=F32
        )
        sc[block] = jnp.where(row_id >= col_id, scores, 0.0)
    half = STRETCH // 2

    def one(i, _):
        c = pl.ds(pl.multiple_of(i * TILE, TILE), TILE)
        select = spread(i, TILE)
        lane = lax.broadcasted_iota(jnp.int32, (128, STRETCH), 0)
        group = lax.broadcasted_iota(jnp.int32, (STRETCH, TILE), 1) >> 6
        for block, other in ((0, o1), (1, o2)):
            rows = block_rows(block)
            gate = silu(rounded(acc[rows, c] + dot(other[...], wm[at, c])))
            values = act[rows, c]
            top = jnp.zeros((half, TILE), F32)
            bottom = jnp.zeros((half, TILE), F32)
            for j in range(TILE // 64):
                h = i * (TILE // 64) + j
                pick = jnp.where(((lane & 31) == h) & (lane < 96), 1.0, 0.0).astype(BF)
                cum = dot(cum3[rows, :], pick)
                cum_s = cum_t[block, pl.ds(h, 1), :]
                step_s = step_t[block, pl.ds(h, 1), :]
                mine = jnp.where(group == j, values, jnp.zeros_like(values))
                m_top = (
                    sc[block, :half, :half]
                    * jnp.exp2(jnp.minimum(cum[:half, :half] - cum_s[:, :half], 0.0))
                    * step_s[:, :half]
                ).astype(BF)
                m_bottom = (
                    sc[block, half:, :]
                    * jnp.exp2(jnp.minimum(cum[half:, :] - cum_s, 0.0))
                    * step_s
                ).astype(BF)
                top = top + dot(m_top, mine[:half, :])
                bottom = bottom + dot(m_bottom, mine)
            within = jnp.concatenate([top, bottom], axis=0)
            p_out[rows, c] = (within + skip[0:1, c] * values.astype(F32)) * gate
            q_out[rows, c] = dot(ecum3[rows, :], select) * gate
        return 0

    lax.fori_loop(0, act.shape[1] // TILE, one, 0)


def mix_part(ids, o1, o2, wm, acc, act, bc, cum3, cum_t, step_t, ecum3, skip):
    return call(
        mix_body,
        [shape(act.shape)] * 2,
        (ids, o1, o2, wm, acc, act, bc, cum3, cum_t, step_t, ecum3, skip),
        "mix_part",
        8e9,
        exps=20 * 512 * 256,
        scratch=[pltpu.VMEM((2, STRETCH, STRETCH), F32)],
    )


def gated_body(
    ids, p, q, bc, got1, got2, state0, rows_in, gain, wo, z, far_r, far_l, squares
):
    carry0 = jnp.where(ids[4] > 0, 1.0, 0.0)
    carry1 = jnp.where(ids[5] > 0, 1.0, 0.0)
    sums = [None, None]
    for j in range(5):
        c = wide(j)
        more = got1[128:, c].astype(F32)
        decay = more[0:1, :] + more[1:2, :] + more[2:3, :]
        entering = got1[:128, c].astype(F32) + decay * got2[:, c].astype(F32)
        start0 = entering * carry0
        start1 = (rows_in[0:1, c] * start0 + state0[:, c]) * carry1
        for block, start in ((0, start0), (1, start1)):
            rows = block_rows(block)
            from_start = dot(bc[rows, 128:], start.astype(BF))
            gated = p[rows, c] + q[rows, c] * from_start
            square = gated * gated
            square = square[:, :128] + square[:, 128:]
            sums[block] = square if sums[block] is None else sums[block] + square
            z[rows, c] = (gated * gain[0:1, c]).astype(BF)
    ncol = wo.shape[1] // RING
    at = pl.ds(pl.multiple_of(ids[3] * ncol, 128), ncol)
    far_r[:STRETCH, :] = dot(z[:STRETCH, :], wo[:, at]).astype(BF)
    far_l[:STRETCH, :] = dot(z[STRETCH:, :], wo[:, at]).astype(BF)
    flats = [jnp.sum(jnp.transpose(s), axis=0, keepdims=True) for s in sums]
    row = lax.broadcasted_iota(jnp.int32, (16, STRETCH), 0)
    for block in range(2):
        squares[:, block_rows(block)] = jnp.broadcast_to(flats[block], (8, STRETCH))
        high, mid, low = split3(flats[block])
        packed = jnp.where(
            row == 0, high, jnp.where(row == 1, mid, jnp.where(row == 2, low, 0.0))
        ).astype(BF)
        far_r[STRETCH:, block_rows(block)] = packed
        far_l[STRETCH:, block_rows(block)] = packed
    far_r[STRETCH:, 512:] = jnp.zeros((16, ncol - 512), BF)
    far_l[STRETCH:, 512:] = jnp.zeros((16, ncol - 512), BF)


def gated_part(ids, p, q, bc, got1, got2, state0, rows_in, gain, wo):
    tok, nv = p.shape
    ncol = wo.shape[1] // RING
    return call(
        gated_body,
        [
            shape((tok, nv), BF),
            shape((STRETCH + 16, ncol), BF),
            shape((STRETCH + 16, ncol), BF),
            shape((8, tok)),
        ],
        (ids, p, q, bc, got1, got2, state0, rows_in, gain, wo),
        "gated_part",
        2 * tok * nv * (ncol + 128),
    )


def near_body(ids, z, wo, low_r, top_l, top_r, low_l):
    ncol = wo.shape[1] // RING
    at_l = pl.ds(pl.multiple_of(ids[1] * ncol, 128), ncol)
    at_r = pl.ds(pl.multiple_of(ids[2] * ncol, 128), ncol)
    low_r[...] = dot(z[STRETCH:, :], wo[:, at_r]).astype(BF)
    top_l[...] = dot(z[:STRETCH, :], wo[:, at_l]).astype(BF)
    top_r[...] = dot(z[:STRETCH, :], wo[:, at_r])
    low_l[...] = dot(z[STRETCH:, :], wo[:, at_l])


def near_part(ids, z, wo):
    tok, nv = z.shape
    ncol = wo.shape[1] // RING
    return call(
        near_body,
        [shape((STRETCH, ncol), BF)] * 2 + [shape((STRETCH, ncol))] * 2,
        (ids, z, wo),
        "near_part",
        4 * tok * nv * ncol,
    )


def mine_body(ids, z, wo, out):
    ncol = wo.shape[1] // RING
    at = pl.ds(pl.multiple_of(ids[0] * ncol, 128), ncol)
    out[...] = dot(z[...], wo[:, at])


def mine_part(ids, z, wo):
    tok, nv = z.shape
    ncol = wo.shape[1] // RING
    return call(mine_body, [shape((tok, ncol))], (ids, z, wo), "mine_part", 2 * tok * nv * ncol)[0]


def add_body(ids, a1, b1, a2, b2, o1, o2):
    o1[:STRETCH, :] = (a1[...] + b1[:STRETCH, :].astype(F32)).astype(BF)
    o1[STRETCH:, :] = b1[STRETCH:, :]
    o2[...] = (a2[...] + b2[:STRETCH, :].astype(F32)).astype(BF)


def add_part(ids, a1, b1, a2, b2):
    return call(
        add_body,
        [shape(b1.shape, BF), shape(a2.shape, BF)],
        (ids, a1, b1, a2, b2),
        "add_part",
        2 * a1.size,
    )


def final_body(ids, own, top_r, low_r, top_l, low_l, mine, sq_r, sq_l, out):
    total = mine[0:1, :]
    for other in (sq_r, sq_l, top_r):
        more = other[STRETCH:, :512].astype(F32)
        total = total + (more[0:1, :] + more[1:2, :] + more[2:3, :])
    inv = lax.rsqrt(total * (1.0 / 5120.0) + 1e-05)
    inv = jnp.transpose(jnp.broadcast_to(inv, (128, inv.shape[1])))
    for block, r, l in ((0, top_r, top_l), (1, low_r, low_l)):
        rows = block_rows(block)
        scale = inv[rows, :]
        for low in range(0, out.shape[1], 128):
            c = slice(low, low + 128)
            value = own[rows, c] + r[:STRETCH, c].astype(F32) + l[:STRETCH, c].astype(F32)
            out[rows, c] = (value * scale).astype(BF)


def final_part(ids, own, top_r, low_r, top_l, low_l, mine, sq_r, sq_l):
    return call(
        final_body,
        [shape(own.shape, BF)],
        (ids, own, top_r, low_r, top_l, low_l, mine, sq_r, sq_l),
        "final_part",
        4 * own.size,
    )[0]


def on_device(
    tokens,
    send_rows,
    send_counts,
    stretch_segments,
    main_proj,
    state_proj,
    step_proj,
    conv_main,
    conv_state,
    step_bias,
    decay_log,
    skip_gain,
    norm_gain,
    out_proj,
):
    ctx = lax.axis_index("ctx").astype(jnp.int32)
    head = lax.axis_index("head").astype(jnp.int32)
    tok, width = tokens.shape
    sources, slots = send_rows.shape[1:]
    heads = step_bias.shape[0]
    inner = main_proj.shape[2]
    head_dim = inner // heads

    send_list = send_rows.reshape(sources * slots)
    pick = (send_list[:, None] == jnp.arange(tok, dtype=jnp.int32)[None, :]).astype(BF)
    outgoing = dot(pick, tokens).astype(BF).reshape(sources, slots, width)
    arrived = lax.all_to_all(outgoing, "ctx", split_axis=0, concat_axis=0, tiled=True)

    blocks = tok // STRETCH
    block_ids = ctx * blocks + jnp.arange(blocks, dtype=jnp.int32)
    segment = jnp.take(stretch_segments, block_ids)
    before = jnp.take(stretch_segments, jnp.maximum(block_ids - 1, 0))
    carry = ((segment == before) & (block_ids > 0)).astype(jnp.int32)
    ring = jnp.stack([head, head + 3, head + 1, head + 2]) % RING
    ids = jnp.concatenate([ring, carry]).astype(jnp.int32)
    wm = main_proj.reshape(main_proj.shape[0], 2 * inner)
    wsd = jnp.concatenate(
        [state_proj, jnp.pad(step_proj, ((0, 0), (0, 128 - heads)))], axis=1
    )
    head_rows = jnp.zeros((8, 128), F32)
    head_rows = head_rows.at[0, :heads].set(step_bias).at[1, :heads].set(jnp.exp(decay_log))
    skip = jnp.broadcast_to(jnp.repeat(skip_gain, head_dim)[None, :], (8, inner))
    gain = jnp.broadcast_to(norm_gain[None, :], (8, inner))

    column = jnp.take(send_counts, ctx, axis=1)
    ends = jnp.cumsum(column)
    begins = ends - column
    position = jnp.arange(tok, dtype=jnp.int32)
    slot = position[:, None] - begins[None, :]
    inside = (slot >= 0) & (slot < column[None, :])
    flat = jnp.sum(
        jnp.where(inside, slot + jnp.arange(sources, dtype=jnp.int32)[None, :] * slots, 0), axis=1
    )
    place = (flat[:, None] == jnp.arange(sources * slots, dtype=jnp.int32)[None, :]).astype(BF)
    arrived, wm, wsd, place = lax.optimization_barrier((arrived, wm, wsd, place))
    packed = dot(place, arrived.reshape(sources * slots, width)).astype(BF)

    r = turned(packed, 1)
    l = turned(packed, -1)
    t = shifted(packed[tok - TAIL :], 1)
    t_r = turned(t, 1)
    t_l = turned(t, -1)
    t_o = turned(t, 2)
    acc = own_part(ids, packed, wsd, wm)
    r, l, acc = lax.optimization_barrier((r, l, acc))
    o1 = turned(r[:STRETCH], 1)
    o2 = turned(l[STRETCH:], -1)
    acc = next_part(ids, r, l, wsd, wm, acc)
    tail = tail_part(ids, t, t_r, t_l, t_o, wsd, wm)
    o1, o2, acc, tail, skip, gain = lax.optimization_barrier((o1, o2, acc, tail, skip, gain))
    act, bc, cum3, cum_t, step_t, ecum3, state0, state_dev, rows_out, payload = state_part(
        ids, o1, o2, wsd, wm, acc, tail, conv_state, conv_main, head_rows
    )

    got1 = shifted(payload, 1)
    joined = join_part(ids, state_dev, rows_out, got1)
    got2 = shifted(joined, 2)
    p, q = mix_part(ids, o1, o2, wm, acc, act, bc, cum3, cum_t, step_t, ecum3, skip)

    z, far_r, far_l, squares = gated_part(
        ids, p, q, bc, got1, got2, state0, rows_out, gain, out_proj
    )
    got_r = turned(far_r, 1)
    got_l = turned(far_l, -1)
    low_r, top_l, top_r, low_l = near_part(ids, z, out_proj)
    low_r = turned(low_r, 1)
    top_l = turned(top_l, -1)
    sum_r, sum_l = add_part(ids, top_r, got_r, low_l, got_l)
    top_r = turned(sum_r, 1)
    low_l = turned(sum_l, -1)
    own = mine_part(ids, z, out_proj)
    return final_part(ids, own, top_r, low_r, top_l, low_l, squares, got_r, got_l)


def solution(mesh):
    return jax.shard_map(
        on_device,
        mesh=mesh,
        in_specs=(
            P("ctx", "head"),
            P("ctx", None, None),
            P(),
            P(),
            P(None, None, "head"),
            P(),
            P(None, "head"),
            P(None, "head"),
            P(),
            P("head"),
            P("head"),
            P("head"),
            P("head"),
            P("head", None),
        ),
        out_specs=P("ctx", "head"),
        check_vma=False,
    )
```

```python
import jax
import jax.numpy as jnp
from jax import lax
from jax.experimental import pallas as pl
from jax.experimental.pallas import tpu as pltpu
from jax.sharding import PartitionSpec as P

BF = jnp.bfloat16
F32 = jnp.float32
STRETCH = 256
TAIL = 16
TILE = 256
LOG2E = 1.4426950408889634
RING = 4
VMEM = 16 * 1024 * 1024


def dot(a, b):
    return jnp.dot(a, b, preferred_element_type=F32)


def turned(value, steps):
    return lax.ppermute(value, "head", [(i, (i + steps) % RING) for i in range(RING)])


def shifted(value, steps):
    count = lax.axis_size("ctx")
    return lax.ppermute(value, "ctx", [(i, i + steps) for i in range(count - steps)])


def silu(v):
    return v * (1.0 / (1.0 + jnp.exp(-v)))


def split3(x):
    high = x.astype(BF).astype(F32)
    rest = x - high
    mid = rest.astype(BF).astype(F32)
    low = (rest - mid).astype(BF).astype(F32)
    return high, mid, low


def pack3(x):
    high, mid, low = split3(x)
    return (high + pltpu.roll(mid, 32, 1) + pltpu.roll(low, 64, 1)).astype(BF)


def spread(tile, width):
    lane = lax.broadcasted_iota(jnp.int32, (128, width), 0)
    col = lax.broadcasted_iota(jnp.int32, (128, width), 1)
    hit = ((lane & 31) == tile * (width // 64) + (col >> 6)) & (lane < 96)
    return jnp.where(hit, 1.0, 0.0).astype(BF)


def call(body, outs, args, name, flops, exps=0, scratch=()):
    size = sum(a.size * a.dtype.itemsize for a in args[1:]) + sum(
        o.size * o.dtype.itemsize for o in outs
    )
    return pl.pallas_call(
        body,
        in_specs=[pl.BlockSpec(memory_space=pltpu.SMEM)]
        + [pl.BlockSpec(memory_space=pltpu.VMEM)] * (len(args) - 1),
        out_specs=[pl.BlockSpec(memory_space=pltpu.VMEM)] * len(outs),
        out_shape=outs,
        scratch_shapes=scratch,
        compiler_params=pltpu.CompilerParams(vmem_limit_bytes=VMEM),
        cost_estimate=pl.CostEstimate(
            flops=int(flops), bytes_accessed=int(size), transcendentals=int(exps)
        ),
        name=name,
    )(*args)


def shape(dims, dtype=F32):
    return jax.ShapeDtypeStruct(dims, dtype)


def chunk_of(ids, at, k):
    return pl.ds(pl.multiple_of(ids[at] * k, 128), k)


def wide(j):
    return slice(j * TILE, (j + 1) * TILE)


def block_rows(block):
    return slice(block * STRETCH, (block + 1) * STRETCH)


def flat_body(ids, w, out):
    k = w.shape[0]
    for low in range(0, k, STRETCH):
        rows = slice(low, low + STRETCH)
        out[rows, :] = w[rows].reshape(STRETCH, out.shape[1])


def flat_part(ids, w):
    out = shape((w.shape[0], 2 * w.shape[2]), BF)
    return call(flat_body, [out], (ids, w), "flat_part", 1e9)[0]


CUT = STRETCH - TAIL


def arrange_body(ids, target, arrived, second, first, last):
    slots = arrived.shape[0]
    for low, high in ((CUT, 2 * STRETCH), (0, CUT)):
        row = lax.broadcasted_iota(jnp.int32, (high - low, slots), 0) + low
        pick = jnp.where(row == target[...], 1.0, 0.0).astype(BF)
        rows = dot(pick, arrived[...]).astype(BF)
        if low:
            second[...] = rows
            last[...] = rows[high - low - TAIL :, :]
        else:
            first[...] = rows


def arrange_part(ids, target, arrived):
    slots, k = arrived.shape
    return call(
        arrange_body,
        [shape((STRETCH + TAIL, k), BF), shape((CUT, k), BF), shape((TAIL, k), BF)],
        (ids, target, arrived),
        "arrange_part",
        2 * 512 * slots * k,
    )


def own_body(ids, x, sp, tp, wm, acc):
    at = chunk_of(ids, 0, x.shape[1])
    acc[:, 2560:2816] = dot(x[...], sp[at, :])
    acc[:, 2816 : 2816 + tp.shape[1]] = dot(x[...], tp[at, :])
    for j in range(10):
        acc[:, wide(j)] = dot(x[...], wm[at, wide(j)])


def own_part(ids, x, sp, tp, wm):
    rows, k = x.shape
    n = 2944
    return call(own_body, [shape((rows, n))], (ids, x, sp, tp, wm), "own_part", 2 * rows * k * n)[0]


def next_body(ids, r, l, sp, tp, wm, before, acc):
    k = r.shape[1]
    at_r, at_l = chunk_of(ids, 1, k), chunk_of(ids, 2, k)
    c = slice(2560, 2816)
    acc[:, c] = before[:, c] + dot(r[...], sp[at_r, :]) + dot(l[...], sp[at_l, :])
    c = slice(2816, 2816 + tp.shape[1])
    acc[:, c] = before[:, c] + dot(r[...], tp[at_r, :]) + dot(l[...], tp[at_l, :])
    for j in range(10):
        c = wide(j)
        acc[:, c] = before[:, c] + dot(r[...], wm[at_r, c]) + dot(l[...], wm[at_l, c])


def next_part(ids, r, l, sp, tp, wm, acc):
    rows, k = r.shape
    n = acc.shape[1]
    return call(
        next_body, [shape((rows, n))], (ids, r, l, sp, tp, wm, acc), "next_part", 4 * rows * k * n
    )[0]


def rounded(x):
    return x.astype(BF).astype(F32)


def conv_silu(xs, taps):
    total = None
    for k in range(4):
        term = xs[5 + k : 5 + k + STRETCH, :] * taps[k : k + 1, :]
        total = term if total is None else total + term
    return silu(total).astype(BF)


def step_rows(row, value):
    high, mid, low = split3(value)
    return jnp.where(row == 0, high, jnp.where(row == 1, mid, jnp.where(row == 2, low, 0.0)))


def decays(raw, heads, cum3, cum_t, step_t, ecum3):
    lane = lax.broadcasted_iota(jnp.int32, (STRETCH, 128), 1)
    row_id = lax.broadcasted_iota(jnp.int32, (STRETCH, STRETCH), 0)
    col_id = lax.broadcasted_iota(jnp.int32, (STRETCH, STRETCH), 1)
    below = jnp.where(row_id >= col_id, 1.0, 0.0).astype(BF)
    raw = jnp.where(lane < 20, raw, 0.0) + heads[0:1, :]
    small = jnp.exp(-jnp.abs(raw))
    one = 1.0 + small
    log_one = jnp.where(one == 1.0, small, jnp.log(one) * (small / (one - 1.0 + 1e-30)))
    step = jnp.where(lane < 20, jnp.maximum(raw, 0.0) + log_one, 0.0)
    sums = dot(below, pack3(step * (heads[1:2, :] * (-LOG2E))))
    sums = sums + pltpu.roll(sums, 96, 1) + pltpu.roll(sums, 64, 1)
    sums = jnp.where(lane < 32, sums, 0.0)
    final = sums[STRETCH - 1 : STRETCH, :]
    cum3[...] = pack3(sums)
    cum_t[...] = jnp.transpose(sums)[:32]
    step_t[...] = jnp.transpose(step)[:32]
    ecum3[...] = pack3(jnp.where(lane < 32, jnp.exp2(sums), 0.0))
    weights = pack3(jnp.exp2(final - sums) * step)
    ends = pack3(jnp.broadcast_to(jnp.where(lane[:1] < 32, jnp.exp2(final), 0.0), (16, 128)))
    return weights, ends


def second_body(
    ids, o1, o2, sp, tp, wm, acc, taps_s, taps_v, heads,
    act, bc, cum3, cum_t, step_t, ecum3, payload, mid, mid_step, xs,
):
    k = o1.shape[1]
    n1 = o1.shape[0]
    at = chunk_of(ids, 3, k)

    def channels(slot, c, w):
        buf = xs.at[slot]
        first = rounded(acc[:n1, c] + dot(o1[...], w))
        buf[8 : n1 - 8, :] = first[TAIL:, :]
        buf[:8, :] = jnp.where(ids[5] > 0, first[8:TAIL, :], 0.0)
        buf[n1 - 8 : STRETCH + 8, :] = rounded(acc[n1:, c] + dot(o2[...], w))
        return buf, first[:TAIL, :]

    buf, edge = channels(0, slice(2560, 2816), sp[at, :])
    mid[:, 1280:] = edge
    bc[...] = conv_silu(buf, taps_s)
    bt = jnp.transpose(bc[:, :128].astype(F32)).astype(BF)
    n = tp.shape[1]
    buf = xs.at[3]
    buf[:n1, :n] = acc[:n1, 2816 : 2816 + n] + dot(o1[...], tp[at, :])
    buf[n1:, :n] = acc[n1:, 2816 : 2816 + n] + dot(o2[...], tp[at, :])
    mid_step[...] = buf[:TAIL, :128]
    weights, ends = decays(buf[TAIL : TAIL + STRETCH, :128], heads, cum3, cum_t, step_t, ecum3)
    carry = jnp.where(ids[5] > 0, 1.0, 0.0)
    row = lax.broadcasted_iota(jnp.int32, (16, TILE), 0)
    for j in range(5):
        c = wide(j)
        buf, edge = channels(1 + j % 2, wide(5 + j), wm[at, wide(5 + j)])
        mid[:, c] = edge
        value = conv_silu(buf, taps_v[:, c])
        act[:, c] = value
        select = spread(j, TILE)
        weighted = (value.astype(F32) * dot(weights, select)).astype(BF)
        payload[:128, c] = dot(bt, weighted).astype(BF)
        payload[128:, c] = step_rows(row, dot(ends, select) * carry).astype(BF)


def block_outs():
    return [
        shape((STRETCH, 1280), BF),
        shape((STRETCH, 256), BF),
        shape((STRETCH, 128), BF),
        shape((32, STRETCH)),
        shape((32, STRETCH)),
        shape((STRETCH, 128), BF),
    ]


def second_part(ids, o1, o2, sp, tp, wm, acc, taps_s, taps_v, heads):
    return call(
        second_body,
        block_outs() + [shape((144, 1280), BF), shape((TAIL, 1536)), shape((TAIL, 128))],
        (ids, o1, o2, sp, tp, wm, acc, taps_s, taps_v, heads),
        "second_part",
        4 * STRETCH * 640 * 1664,
        scratch=[pltpu.VMEM((4, STRETCH + TAIL, TILE), F32)],
    )


def first_body(
    ids, o1, o2, sp, tp, wm, acc, taps_s, taps_v, heads, mid, mid_step, got,
    act, bc, cum3, cum_t, step_t, ecum3, joined, joined_low, state0, end_row, xs,
):
    k = o1.shape[1]
    n1 = o1.shape[0]
    at = chunk_of(ids, 3, k)

    def channels(slot, c, w, edge):
        buf = xs.at[slot]
        first = rounded(acc[:n1, c] + dot(o1[...], w))
        buf[8 : n1 - 8, :] = first[TAIL:, :]
        buf[:8, :] = jnp.where(ids[4] > 0, first[8:TAIL, :], 0.0)
        buf[n1 - 8 : STRETCH - 8, :] = rounded(acc[n1:, c] + dot(o2[...], w))
        buf[STRETCH - 8 : STRETCH + 8, :] = edge
        return buf

    buf = channels(0, slice(2560, 2816), sp[at, :], mid[:, 1280:])
    bc[...] = conv_silu(buf, taps_s)
    bt = jnp.transpose(bc[:, :128].astype(F32)).astype(BF)
    n = tp.shape[1]
    buf = xs.at[3]
    buf[:n1, :n] = acc[:n1, 2816 : 2816 + n] + dot(o1[...], tp[at, :])
    buf[n1:STRETCH, :n] = acc[n1:, 2816 : 2816 + n] + dot(o2[...], tp[at, :])
    buf[STRETCH:, :128] = mid_step[...]
    weights, ends = decays(buf[TAIL : TAIL + STRETCH, :128], heads, cum3, cum_t, step_t, ecum3)
    carry = jnp.where(ids[4] > 0, 1.0, 0.0)
    row = lax.broadcasted_iota(jnp.int32, (16, TILE), 0)
    for j in range(5):
        c = wide(j)
        buf = channels(1 + j % 2, wide(5 + j), wm[at, wide(5 + j)], mid[:, c])
        value = conv_silu(buf, taps_v[:, c])
        act[:, c] = value
        select = spread(j, TILE)
        weighted = (value.astype(F32) * dot(weights, select)).astype(BF)
        state = dot(bt, weighted)
        end = dot(ends, select)
        state0[:, c] = state
        end_row[:, c] = end[:8, :]
        decay = end[0:1, :] * carry
        more = got[128:, c].astype(F32)
        before = more[0:1, :] + more[1:2, :] + more[2:3, :]
        low = (state + decay * got[:128, c].astype(F32)).astype(BF)
        joined[:128, c] = low
        joined_low[:, c] = low
        joined[128:, c] = step_rows(row, decay * before).astype(BF)


def first_part(ids, o1, o2, sp, tp, wm, acc, taps_s, taps_v, heads, mid, mid_step, got):
    return call(
        first_body,
        block_outs()
        + [shape((144, 1280), BF), shape((128, 1280), BF), shape((128, 1280)), shape((8, 1280))],
        (ids, o1, o2, sp, tp, wm, acc, taps_s, taps_v, heads, mid, mid_step, got),
        "first_part",
        4 * STRETCH * 640 * 1664,
        scratch=[pltpu.VMEM((4, STRETCH + TAIL, TILE), F32)],
    )


def mix_body(
    ids, a1, a2, b1, b2, wm, acc0, acc1, heads,
    act0, bc0, cum30, cum_t0, step_t0, ecum30,
    act1, bc1, cum31, cum_t1, step_t1, ecum31,
    p_out, q_out, sc, xo,
):
    k = a1.shape[1]
    at = chunk_of(ids, 3, k)
    low = 0
    for piece in (a1[TAIL:, :], a2[...], b1[...], b2[...]):
        xo[low : low + piece.shape[0], :] = piece
        low += piece.shape[0]
    row_id = lax.broadcasted_iota(jnp.int32, (STRETCH, STRETCH), 0)
    col_id = lax.broadcasted_iota(jnp.int32, (STRETCH, STRETCH), 1)
    for block, bc in ((0, bc0), (1, bc1)):
        scores = lax.dot_general(
            bc[:, 128:], bc[:, :128], (((1,), (1,)), ((), ())), preferred_element_type=F32
        )
        sc[block] = jnp.where(row_id >= col_id, scores, 0.0)
    half = STRETCH // 2
    heads3 = pack3(heads[...])

    def one(i, _):
        c = pl.ds(pl.multiple_of(i * TILE, TILE), TILE)
        select = spread(i, TILE)
        skip = dot(heads3, select)[2:3, :]
        lane = lax.broadcasted_iota(jnp.int32, (128, STRETCH), 0)
        group = lax.broadcasted_iota(jnp.int32, (STRETCH, TILE), 1) >> 6
        for block, act, cum3, cum_t, step_t, ecum3 in (
            (1, act1, cum31, cum_t1, step_t1, ecum31),
            (0, act0, cum30, cum_t0, step_t0, ecum30),
        ):
            rows = block_rows(block)
            if block:
                gate = acc1[TAIL:, c]
            else:
                gate = jnp.concatenate([acc0[TAIL:, c], acc1[:TAIL, c]], axis=0)
            gate = silu(rounded(gate + dot(xo[rows, :], wm[at, c])))
            values = act[:, c]
            top = jnp.zeros((half, TILE), F32)
            bottom = jnp.zeros((half, TILE), F32)
            for j in range(TILE // 64):
                h = i * (TILE // 64) + j
                pick = jnp.where(((lane & 31) == h) & (lane < 96), 1.0, 0.0).astype(BF)
                cum = dot(cum3[...], pick)
                cum_s = cum_t[pl.ds(h, 1), :]
                step_s = step_t[pl.ds(h, 1), :]
                mine = jnp.where(group == j, values, jnp.zeros_like(values))
                m_top = (
                    sc[block, :half, :half]
                    * jnp.exp2(jnp.minimum(cum[:half, :half] - cum_s[:, :half], 0.0))
                    * step_s[:, :half]
                ).astype(BF)
                m_bottom = (
                    sc[block, half:, :]
                    * jnp.exp2(jnp.minimum(cum[half:, :] - cum_s, 0.0))
                    * step_s
                ).astype(BF)
                top = top + dot(m_top, mine[:half, :])
                bottom = bottom + dot(m_bottom, mine)
            within = jnp.concatenate([top, bottom], axis=0)
            p_out[rows, c] = (within + skip * values.astype(F32)) * gate
            q_out[rows, c] = dot(ecum3[...], select) * gate
        return 0

    lax.fori_loop(0, act0.shape[1] // TILE, one, 0)


def mix_part(ids, a1, a2, b1, b2, wm, acc0, acc1, heads, block0, block1):
    tok = 2 * STRETCH
    return call(
        mix_body,
        [shape((tok, 1280))] * 2,
        (ids, a1, a2, b1, b2, wm, acc0, acc1, heads, *block0, *block1),
        "mix_part",
        8e9,
        exps=20 * 512 * 256,
        scratch=[pltpu.VMEM((2, STRETCH, STRETCH), F32), pltpu.VMEM((tok, a1.shape[1]), BF)],
    )


def gated_body(
    ids, p, q, bc0, bc1, got_s, got_v, got_w, state0, end_row, gain, wo,
    z, far_r, far_l, dir_r, dir_l, squares,
):
    carry0 = jnp.where(ids[4] > 0, 1.0, 0.0)
    carry1 = jnp.where(ids[5] > 0, 1.0, 0.0)
    sums = [None, None]
    for j in range(5):
        c = wide(j)
        more = got_s[128:, c].astype(F32)
        decay1 = more[0:1, :] + more[1:2, :] + more[2:3, :]
        more = got_v[128:, c].astype(F32)
        decay2 = more[0:1, :] + more[1:2, :] + more[2:3, :]
        entering = got_s[:128, c].astype(F32) + decay1 * (
            got_v[:128, c].astype(F32) + decay2 * got_w[:, c].astype(F32)
        )
        start0 = entering * carry0
        start1 = (end_row[0:1, c] * start0 + state0[:, c]) * carry1
        for block, start, bc in ((0, start0, bc0), (1, start1, bc1)):
            rows = block_rows(block)
            from_start = dot(bc[:, 128:], start.astype(BF))
            gated = p[rows, c] + q[rows, c] * from_start
            square = gated * gated
            square = square[:, :128] + square[:, 128:]
            sums[block] = square if sums[block] is None else sums[block] + square
            z[rows, c] = (gated * gain[0:1, c]).astype(BF)
    ncol = wo.shape[1] // RING
    top, low = block_rows(0), block_rows(1)
    far_r[:STRETCH, :] = dot(z[top, :], wo[:, chunk_of(ids, 3, ncol)]).astype(BF)
    far_l[:STRETCH, :] = dot(z[low, :], wo[:, chunk_of(ids, 3, ncol)]).astype(BF)
    dir_r[...] = dot(z[low, :], wo[:, chunk_of(ids, 2, ncol)]).astype(BF)
    dir_l[...] = dot(z[top, :], wo[:, chunk_of(ids, 1, ncol)]).astype(BF)
    row = lax.broadcasted_iota(jnp.int32, (16, STRETCH), 0)
    for block in range(2):
        c = block_rows(block)
        flat = jnp.sum(jnp.transpose(sums[block]), axis=0, keepdims=True)
        squares[:, c] = jnp.broadcast_to(flat, (8, STRETCH))
        packed = step_rows(row, flat).astype(BF)
        far_r[STRETCH:, c] = packed
        far_l[STRETCH:, c] = packed
    far_r[STRETCH:, 512:] = jnp.zeros((16, ncol - 512), BF)
    far_l[STRETCH:, 512:] = jnp.zeros((16, ncol - 512), BF)


def gated_part(ids, p, q, bc0, bc1, got_s, got_v, got_w, state0, end_row, gain, wo):
    tok, nv = p.shape
    ncol = wo.shape[1] // RING
    return call(
        gated_body,
        [
            shape((tok, nv), BF),
            shape((STRETCH + 16, ncol), BF),
            shape((STRETCH + 16, ncol), BF),
            shape((STRETCH, ncol), BF),
            shape((STRETCH, ncol), BF),
            shape((8, tok)),
        ],
        (ids, p, q, bc0, bc1, got_s, got_v, got_w, state0, end_row, gain, wo),
        "gated_part",
        2 * tok * nv * (2 * ncol + 128),
    )


def near_body(ids, z, wo, top_r, low_l):
    ncol = wo.shape[1] // RING
    top_r[...] = dot(z[:STRETCH, :], wo[:, chunk_of(ids, 2, ncol)])
    low_l[...] = dot(z[STRETCH:, :], wo[:, chunk_of(ids, 1, ncol)])


def near_part(ids, z, wo):
    tok, nv = z.shape
    ncol = wo.shape[1] // RING
    return call(
        near_body, [shape((STRETCH, ncol))] * 2, (ids, z, wo), "near_part", 2 * tok * nv * ncol
    )


def mine_body(ids, z, wo, low_r, top_l, own):
    ncol = wo.shape[1] // RING
    at = chunk_of(ids, 0, ncol)
    own[:STRETCH, :] = dot(z[:STRETCH, :], wo[:, at]) + top_l[...].astype(F32)
    own[STRETCH:, :] = dot(z[STRETCH:, :], wo[:, at]) + low_r[...].astype(F32)


def mine_part(ids, z, wo, low_r, top_l):
    tok, nv = z.shape
    ncol = wo.shape[1] // RING
    return call(
        mine_body,
        [shape((tok, ncol))],
        (ids, z, wo, low_r, top_l),
        "mine_part",
        4 * tok * nv * ncol,
    )[0]


def add_body(ids, a1, b1, a2, b2, o1, o2):
    o1[:STRETCH, :] = (a1[...] + b1[:STRETCH, :].astype(F32)).astype(BF)
    o1[STRETCH:, :] = b1[STRETCH:, :]
    o2[...] = (a2[...] + b2[:STRETCH, :].astype(F32)).astype(BF)


def add_part(ids, a1, b1, a2, b2):
    return call(
        add_body,
        [shape(b1.shape, BF), shape(a2.shape, BF)],
        (ids, a1, b1, a2, b2),
        "add_part",
        2 * a1.size,
    )


def final_body(ids, own, top_r, low_l, mine, sq_r, sq_l, out):
    total = mine[0:1, :]
    for other in (sq_r, sq_l, top_r):
        more = other[STRETCH:, :512].astype(F32)
        total = total + (more[0:1, :] + more[1:2, :] + more[2:3, :])
    inv = lax.rsqrt(total * (1.0 / 5120.0) + 1e-05)
    inv = jnp.transpose(jnp.broadcast_to(inv, (128, inv.shape[1])))
    for block, got in ((0, top_r), (1, low_l)):
        rows = block_rows(block)
        scale = inv[rows, :]
        for low in range(0, out.shape[1], 128):
            c = slice(low, low + 128)
            out[rows, c] = ((own[rows, c] + got[:STRETCH, c].astype(F32)) * scale).astype(BF)


def final_part(ids, own, top_r, low_l, mine, sq_r, sq_l):
    return call(
        final_body,
        [shape(own.shape, BF)],
        (ids, own, top_r, low_l, mine, sq_r, sq_l),
        "final_part",
        4 * own.size,
    )[0]


def on_device(
    tokens,
    send_rows,
    send_counts,
    stretch_segments,
    main_proj,
    state_proj,
    step_proj,
    conv_main,
    conv_state,
    step_bias,
    decay_log,
    skip_gain,
    norm_gain,
    out_proj,
):
    ctx = lax.axis_index("ctx").astype(jnp.int32)
    head = lax.axis_index("head").astype(jnp.int32)
    tok, width = tokens.shape
    sources, slots = send_rows.shape[1:]
    heads = step_bias.shape[0]
    inner = main_proj.shape[2]
    head_dim = inner // heads

    send_list = send_rows.reshape(sources * slots)
    pick = (send_list[:, None] == jnp.arange(tok, dtype=jnp.int32)[None, :]).astype(BF)
    outgoing = dot(pick, tokens).astype(BF).reshape(sources, slots, width)
    arrived = lax.all_to_all(outgoing, "ctx", split_axis=0, concat_axis=0, tiled=True)

    blocks = tok // STRETCH
    block_ids = ctx * blocks + jnp.arange(blocks, dtype=jnp.int32)
    segment = jnp.take(stretch_segments, block_ids)
    before = jnp.take(stretch_segments, jnp.maximum(block_ids - 1, 0))
    carry = ((segment == before) & (block_ids > 0)).astype(jnp.int32)
    ring = jnp.stack([head, head + 3, head + 1, head + 2]) % RING
    ids = jnp.concatenate([ring, carry]).astype(jnp.int32)
    wm = flat_part(ids, main_proj)
    pad = ((0, 128 - heads),)
    head_rows = jnp.stack(
        [jnp.pad(step_bias, pad), jnp.pad(jnp.exp(decay_log), pad), jnp.pad(skip_gain, pad)]
    )
    head_rows = jnp.pad(head_rows, ((0, 5), (0, 0)))
    gain = norm_gain[None, :]

    column = jnp.take(send_counts, ctx, axis=1)
    begins = jnp.cumsum(column) - column
    slot = jnp.arange(slots, dtype=jnp.int32)[None, :]
    target = jnp.where(slot < column[:, None], begins[:, None] + slot, -1)
    target = target.reshape(1, sources * slots)
    arrived, wm, target, head_rows, gain, ids = lax.optimization_barrier(
        (arrived, wm, target, head_rows, gain, ids)
    )
    second, first, last = arrange_part(ids, target, arrived.reshape(sources * slots, width))
    weights = (state_proj, step_proj, wm)
    taps = (conv_state, conv_main, head_rows)

    r1 = turned(second, 1)
    l1 = turned(second, -1)
    t = shifted(last, 1)
    acc1 = own_part(ids, second, *weights)
    first = jnp.concatenate([t, first], axis=0)
    r1, l1, acc1, first = lax.optimization_barrier((r1, l1, acc1, first))
    cut = STRETCH // 2 + TAIL
    b1 = turned(r1[:cut], 1)
    b2 = turned(l1[cut:], -1)
    acc1 = next_part(ids, r1, l1, *weights, acc1)
    first, acc1 = lax.optimization_barrier((first, acc1))
    r0 = turned(first, 1)
    l0 = turned(first, -1)
    acc0 = own_part(ids, first, *weights)
    b1, b2, acc1, acc0 = lax.optimization_barrier((b1, b2, acc1, acc0))
    *block1, payload, mid, mid_step = second_part(ids, b1, b2, *weights, acc1, *taps)
    got_s = shifted(payload, 1)
    r0, l0, acc0, payload = lax.optimization_barrier((r0, l0, acc0, payload))
    cut = STRETCH // 2
    a1 = turned(r0[:cut], 1)
    a2 = turned(l0[cut:], -1)
    acc0 = next_part(ids, r0, l0, *weights, acc0)
    *block0, joined, joined_low, state0, end_row = first_part(
        ids, a1, a2, *weights, acc0, *taps, mid, mid_step, got_s
    )

    got_v = shifted(joined, 1)
    got_w = shifted(joined_low, 2)
    p, q = mix_part(ids, a1, a2, b1, b2, wm, acc0, acc1, head_rows, block0, block1)

    z, far_r, far_l, dir_r, dir_l, squares = gated_part(
        ids, p, q, block0[1], block1[1], got_s, got_v, got_w, state0, end_row, gain, out_proj
    )
    got_r = turned(far_r, 1)
    got_l = turned(far_l, -1)
    low_r = turned(dir_r, 1)
    top_l = turned(dir_l, -1)
    top_r, low_l = near_part(ids, z, out_proj)
    sum_r, sum_l = add_part(ids, top_r, got_r, low_l, got_l)
    top_r = turned(sum_r, 1)
    low_l = turned(sum_l, -1)
    own = mine_part(ids, z, out_proj, low_r, top_l)
    return final_part(ids, own, top_r, low_l, squares, got_r, got_l)


def solution(mesh):
    return jax.shard_map(
        on_device,
        mesh=mesh,
        in_specs=(
            P("ctx", "head"),
            P("ctx", None, None),
            P(),
            P(),
            P(None, None, "head"),
            P(),
            P(None, "head"),
            P(None, "head"),
            P(),
            P("head"),
            P("head"),
            P("head"),
            P("head"),
            P("head", None),
        ),
        out_specs=P("ctx", "head"),
        check_vma=False,
    )
```

```python
import jax
import jax.numpy as jnp
from jax import lax
from jax.experimental import pallas as pl
from jax.experimental.pallas import tpu as pltpu
from jax.sharding import PartitionSpec as P

BF = jnp.bfloat16
F32 = jnp.float32
STRETCH = 256
TAIL = 16
TILE = 256
LOG2E = 1.4426950408889634
RING = 4
VMEM = 16 * 1024 * 1024


def dot(a, b):
    return jnp.dot(a, b, preferred_element_type=F32)


def turned(value, steps):
    return lax.ppermute(value, "head", [(i, (i + steps) % RING) for i in range(RING)])


def shifted(value, steps):
    count = lax.axis_size("ctx")
    return lax.ppermute(value, "ctx", [(i, i + steps) for i in range(count - steps)])


def silu(v):
    return v * (1.0 / (1.0 + jnp.exp(-v)))


def split3(x):
    high = x.astype(BF).astype(F32)
    rest = x - high
    mid = rest.astype(BF).astype(F32)
    low = (rest - mid).astype(BF).astype(F32)
    return high, mid, low


def pack3(x):
    high, mid, low = split3(x)
    return (high + pltpu.roll(mid, 32, 1) + pltpu.roll(low, 64, 1)).astype(BF)


def spread(tile, width):
    lane = lax.broadcasted_iota(jnp.int32, (128, width), 0)
    col = lax.broadcasted_iota(jnp.int32, (128, width), 1)
    hit = ((lane & 31) == tile * (width // 64) + (col >> 6)) & (lane < 96)
    return jnp.where(hit, 1.0, 0.0).astype(BF)


def call(body, outs, args, name, flops, exps=0, scratch=()):
    size = sum(a.size * a.dtype.itemsize for a in args[1:]) + sum(
        o.size * o.dtype.itemsize for o in outs
    )
    return pl.pallas_call(
        body,
        in_specs=[pl.BlockSpec(memory_space=pltpu.SMEM)]
        + [pl.BlockSpec(memory_space=pltpu.VMEM)] * (len(args) - 1),
        out_specs=[pl.BlockSpec(memory_space=pltpu.VMEM)] * len(outs),
        out_shape=outs,
        scratch_shapes=scratch,
        compiler_params=pltpu.CompilerParams(vmem_limit_bytes=VMEM),
        cost_estimate=pl.CostEstimate(
            flops=int(flops), bytes_accessed=int(size), transcendentals=int(exps)
        ),
        name=name,
    )(*args)


def shape(dims, dtype=F32):
    return jax.ShapeDtypeStruct(dims, dtype)


def chunk_of(ids, at, k):
    return pl.ds(pl.multiple_of(ids[at] * k, 128), k)


def wide(j):
    return slice(j * TILE, (j + 1) * TILE)


def block_rows(block):
    return slice(block * STRETCH, (block + 1) * STRETCH)


def flat_body(ids, w, out):
    k = w.shape[0]
    for low in range(0, k, STRETCH):
        rows = slice(low, low + STRETCH)
        out[rows, :] = w[rows].reshape(STRETCH, out.shape[1])


def flat_part(ids, w):
    out = shape((w.shape[0], 2 * w.shape[2]), BF)
    return call(flat_body, [out], (ids, w), "flat_part", 1e9)[0]


CUT = STRETCH - TAIL


def arrange_body(ids, target, arrived, second, first, last):
    slots = arrived.shape[0]
    for low, high in ((CUT, 2 * STRETCH), (0, CUT)):
        row = lax.broadcasted_iota(jnp.int32, (high - low, slots), 0) + low
        pick = jnp.where(row == target[...], 1.0, 0.0).astype(BF)
        rows = dot(pick, arrived[...]).astype(BF)
        if low:
            second[...] = rows
            last[...] = rows[high - low - TAIL :, :]
        else:
            first[...] = rows


def arrange_part(ids, target, arrived):
    slots, k = arrived.shape
    return call(
        arrange_body,
        [shape((STRETCH + TAIL, k), BF), shape((CUT, k), BF), shape((TAIL, k), BF)],
        (ids, target, arrived),
        "arrange_part",
        2 * 512 * slots * k,
    )


def own_body(ids, x, sp, tp, wm, acc):
    at = chunk_of(ids, 0, x.shape[1])
    acc[:, 2560:2816] = dot(x[...], sp[at, :])
    acc[:, 2816 : 2816 + tp.shape[1]] = dot(x[...], tp[at, :])
    for j in range(10):
        acc[:, wide(j)] = dot(x[...], wm[at, wide(j)])


def own_part(ids, x, sp, tp, wm):
    rows, k = x.shape
    n = 2944
    return call(own_body, [shape((rows, n))], (ids, x, sp, tp, wm), "own_part", 2 * rows * k * n)[0]


def next_body(ids, r, l, sp, tp, wm, before, acc):
    k = r.shape[1]
    at_r, at_l = chunk_of(ids, 1, k), chunk_of(ids, 2, k)
    c = slice(2560, 2816)
    acc[:, c] = before[:, c] + dot(r[...], sp[at_r, :]) + dot(l[...], sp[at_l, :])
    c = slice(2816, 2816 + tp.shape[1])
    acc[:, c] = before[:, c] + dot(r[...], tp[at_r, :]) + dot(l[...], tp[at_l, :])
    for j in range(10):
        c = wide(j)
        acc[:, c] = before[:, c] + dot(r[...], wm[at_r, c]) + dot(l[...], wm[at_l, c])


def next_part(ids, r, l, sp, tp, wm, acc):
    rows, k = r.shape
    n = acc.shape[1]
    return call(
        next_body, [shape((rows, n))], (ids, r, l, sp, tp, wm, acc), "next_part", 4 * rows * k * n
    )[0]


def rounded(x):
    return x.astype(BF).astype(F32)


def conv_silu(xs, taps):
    total = None
    for k in range(4):
        term = xs[5 + k : 5 + k + STRETCH, :] * taps[k : k + 1, :]
        total = term if total is None else total + term
    return silu(total).astype(BF)


def step_rows(row, value):
    high, mid, low = split3(value)
    return jnp.where(row == 0, high, jnp.where(row == 1, mid, jnp.where(row == 2, low, 0.0)))


def decays(raw, heads, cum3, cum_t, step_t, ecum3):
    lane = lax.broadcasted_iota(jnp.int32, (STRETCH, 128), 1)
    row_id = lax.broadcasted_iota(jnp.int32, (STRETCH, STRETCH), 0)
    col_id = lax.broadcasted_iota(jnp.int32, (STRETCH, STRETCH), 1)
    below = jnp.where(row_id >= col_id, 1.0, 0.0).astype(BF)
    raw = jnp.where(lane < 20, raw, 0.0) + heads[0:1, :]
    small = jnp.exp(-jnp.abs(raw))
    one = 1.0 + small
    log_one = jnp.where(one == 1.0, small, jnp.log(one) * (small / (one - 1.0 + 1e-30)))
    step = jnp.where(lane < 20, jnp.maximum(raw, 0.0) + log_one, 0.0)
    sums = dot(below, pack3(step * (heads[1:2, :] * (-LOG2E))))
    sums = sums + pltpu.roll(sums, 96, 1) + pltpu.roll(sums, 64, 1)
    sums = jnp.where(lane < 32, sums, 0.0)
    final = sums[STRETCH - 1 : STRETCH, :]
    cum3[...] = pack3(sums)
    cum_t[...] = jnp.transpose(sums)[:32]
    step_t[...] = jnp.transpose(step)[:32]
    ecum3[...] = pack3(jnp.where(lane < 32, jnp.exp2(sums), 0.0))
    weights = pack3(jnp.exp2(final - sums) * step)
    ends = pack3(jnp.broadcast_to(jnp.where(lane[:1] < 32, jnp.exp2(final), 0.0), (16, 128)))
    return weights, ends


def second_body(
    ids, o1, o2, sp, tp, wm, acc, taps_s, taps_v, heads,
    act, bc, cum3, cum_t, step_t, ecum3, payload, mid, mid_step, xs,
):
    k = o1.shape[1]
    n1 = o1.shape[0]
    at = chunk_of(ids, 3, k)

    def channels(slot, c, w):
        buf = xs.at[slot]
        first = rounded(acc[:n1, c] + dot(o1[...], w))
        buf[8 : n1 - 8, :] = first[TAIL:, :]
        buf[:8, :] = jnp.where(ids[5] > 0, first[8:TAIL, :], 0.0)
        buf[n1 - 8 : STRETCH + 8, :] = rounded(acc[n1:, c] + dot(o2[...], w))
        return buf, first[:TAIL, :]

    buf, edge = channels(0, slice(2560, 2816), sp[at, :])
    mid[:, 1280:] = edge
    bc[...] = conv_silu(buf, taps_s)
    bt = jnp.transpose(bc[:, :128].astype(F32)).astype(BF)
    n = tp.shape[1]
    buf = xs.at[3]
    buf[:n1, :n] = acc[:n1, 2816 : 2816 + n] + dot(o1[...], tp[at, :])
    buf[n1:, :n] = acc[n1:, 2816 : 2816 + n] + dot(o2[...], tp[at, :])
    mid_step[...] = buf[:TAIL, :128]
    weights, ends = decays(buf[TAIL : TAIL + STRETCH, :128], heads, cum3, cum_t, step_t, ecum3)
    carry = jnp.where(ids[5] > 0, 1.0, 0.0)
    row = lax.broadcasted_iota(jnp.int32, (16, TILE), 0)
    for j in range(5):
        c = wide(j)
        buf, edge = channels(1 + j % 2, wide(5 + j), wm[at, wide(5 + j)])
        mid[:, c] = edge
        value = conv_silu(buf, taps_v[:, c])
        act[:, c] = value
        select = spread(j, TILE)
        weighted = (value.astype(F32) * dot(weights, select)).astype(BF)
        payload[:128, c] = dot(bt, weighted).astype(BF)
        payload[128:, c] = step_rows(row, dot(ends, select) * carry).astype(BF)


def block_outs():
    return [
        shape((STRETCH, 1280), BF),
        shape((STRETCH, 256), BF),
        shape((STRETCH, 128), BF),
        shape((32, STRETCH)),
        shape((32, STRETCH)),
        shape((STRETCH, 128), BF),
    ]


def second_part(ids, o1, o2, sp, tp, wm, acc, taps_s, taps_v, heads):
    return call(
        second_body,
        block_outs() + [shape((144, 1280), BF), shape((TAIL, 1536)), shape((TAIL, 128))],
        (ids, o1, o2, sp, tp, wm, acc, taps_s, taps_v, heads),
        "second_part",
        4 * STRETCH * 640 * 1664,
        scratch=[pltpu.VMEM((4, STRETCH + TAIL, TILE), F32)],
    )


def first_body(
    ids, o1, o2, sp, tp, wm, acc, taps_s, taps_v, heads, mid, mid_step, got,
    act, bc, cum3, cum_t, step_t, ecum3, joined, joined_low, state0, end_row, xs,
):
    k = o1.shape[1]
    n1 = o1.shape[0]
    at = chunk_of(ids, 3, k)

    def channels(slot, c, w, edge):
        buf = xs.at[slot]
        first = rounded(acc[:n1, c] + dot(o1[...], w))
        buf[8 : n1 - 8, :] = first[TAIL:, :]
        buf[:8, :] = jnp.where(ids[4] > 0, first[8:TAIL, :], 0.0)
        buf[n1 - 8 : STRETCH - 8, :] = rounded(acc[n1:, c] + dot(o2[...], w))
        buf[STRETCH - 8 : STRETCH + 8, :] = edge
        return buf

    buf = channels(0, slice(2560, 2816), sp[at, :], mid[:, 1280:])
    bc[...] = conv_silu(buf, taps_s)
    bt = jnp.transpose(bc[:, :128].astype(F32)).astype(BF)
    n = tp.shape[1]
    buf = xs.at[3]
    buf[:n1, :n] = acc[:n1, 2816 : 2816 + n] + dot(o1[...], tp[at, :])
    buf[n1:STRETCH, :n] = acc[n1:, 2816 : 2816 + n] + dot(o2[...], tp[at, :])
    buf[STRETCH:, :128] = mid_step[...]
    weights, ends = decays(buf[TAIL : TAIL + STRETCH, :128], heads, cum3, cum_t, step_t, ecum3)
    carry = jnp.where(ids[4] > 0, 1.0, 0.0)
    row = lax.broadcasted_iota(jnp.int32, (16, TILE), 0)
    for j in range(5):
        c = wide(j)
        buf = channels(1 + j % 2, wide(5 + j), wm[at, wide(5 + j)], mid[:, c])
        value = conv_silu(buf, taps_v[:, c])
        act[:, c] = value
        select = spread(j, TILE)
        weighted = (value.astype(F32) * dot(weights, select)).astype(BF)
        state = dot(bt, weighted)
        end = dot(ends, select)
        state0[:, c] = state
        end_row[:, c] = end[:8, :]
        decay = end[0:1, :] * carry
        more = got[128:, c].astype(F32)
        before = more[0:1, :] + more[1:2, :] + more[2:3, :]
        low = (state + decay * got[:128, c].astype(F32)).astype(BF)
        joined[:128, c] = low
        joined_low[:, c] = low
        joined[128:, c] = step_rows(row, decay * before).astype(BF)


def first_part(ids, o1, o2, sp, tp, wm, acc, taps_s, taps_v, heads, mid, mid_step, got):
    return call(
        first_body,
        block_outs()
        + [shape((144, 1280), BF), shape((128, 1280), BF), shape((128, 1280)), shape((8, 1280))],
        (ids, o1, o2, sp, tp, wm, acc, taps_s, taps_v, heads, mid, mid_step, got),
        "first_part",
        4 * STRETCH * 640 * 1664,
        scratch=[pltpu.VMEM((4, STRETCH + TAIL, TILE), F32)],
    )


def mix_body(
    ids, a1, a2, b1, b2, wm, acc0, acc1, heads,
    act0, bc0, cum30, cum_t0, step_t0, ecum30,
    act1, bc1, cum31, cum_t1, step_t1, ecum31,
    p_out, q_out, sc, xo,
):
    k = a1.shape[1]
    at = chunk_of(ids, 3, k)
    low = 0
    for piece in (a1[TAIL:, :], a2[...], b1[...], b2[...]):
        xo[low : low + piece.shape[0], :] = piece
        low += piece.shape[0]
    row_id = lax.broadcasted_iota(jnp.int32, (STRETCH, STRETCH), 0)
    col_id = lax.broadcasted_iota(jnp.int32, (STRETCH, STRETCH), 1)
    for block, bc in ((0, bc0), (1, bc1)):
        scores = lax.dot_general(
            bc[:, 128:], bc[:, :128], (((1,), (1,)), ((), ())), preferred_element_type=F32
        )
        sc[block] = jnp.where(row_id >= col_id, scores, 0.0)
    half = STRETCH // 2
    heads3 = pack3(heads[...])

    def one(i, _):
        c = pl.ds(pl.multiple_of(i * TILE, TILE), TILE)
        select = spread(i, TILE)
        skip = dot(heads3, select)[2:3, :]
        lane = lax.broadcasted_iota(jnp.int32, (128, STRETCH), 0)
        group = lax.broadcasted_iota(jnp.int32, (STRETCH, TILE), 1) >> 6
        for block, act, cum3, cum_t, step_t, ecum3 in (
            (1, act1, cum31, cum_t1, step_t1, ecum31),
            (0, act0, cum30, cum_t0, step_t0, ecum30),
        ):
            rows = block_rows(block)
            if block:
                gate = acc1[TAIL:, c]
            else:
                gate = jnp.concatenate([acc0[TAIL:, c], acc1[:TAIL, c]], axis=0)
            gate = silu(rounded(gate + dot(xo[rows, :], wm[at, c])))
            values = act[:, c]
            top = jnp.zeros((half, TILE), F32)
            bottom = jnp.zeros((half, TILE), F32)
            for j in range(TILE // 64):
                h = i * (TILE // 64) + j
                pick = jnp.where(((lane & 31) == h) & (lane < 96), 1.0, 0.0).astype(BF)
                cum = dot(cum3[...], pick)
                cum_s = cum_t[pl.ds(h, 1), :]
                step_s = step_t[pl.ds(h, 1), :]
                mine = jnp.where(group == j, values, jnp.zeros_like(values))
                m_top = (
                    sc[block, :half, :half]
                    * jnp.exp2(jnp.minimum(cum[:half, :half] - cum_s[:, :half], 0.0))
                    * step_s[:, :half]
                ).astype(BF)
                m_bottom = (
                    sc[block, half:, :]
                    * jnp.exp2(jnp.minimum(cum[half:, :] - cum_s, 0.0))
                    * step_s
                ).astype(BF)
                top = top + dot(m_top, mine[:half, :])
                bottom = bottom + dot(m_bottom, mine)
            within = jnp.concatenate([top, bottom], axis=0)
            p_out[rows, c] = (within + skip * values.astype(F32)) * gate
            q_out[rows, c] = dot(ecum3[...], select) * gate
        return 0

    lax.fori_loop(0, act0.shape[1] // TILE, one, 0)


def mix_part(ids, a1, a2, b1, b2, wm, acc0, acc1, heads, block0, block1):
    tok = 2 * STRETCH
    return call(
        mix_body,
        [shape((tok, 1280))] * 2,
        (ids, a1, a2, b1, b2, wm, acc0, acc1, heads, *block0, *block1),
        "mix_part",
        8e9,
        exps=20 * 512 * 256,
        scratch=[pltpu.VMEM((2, STRETCH, STRETCH), F32), pltpu.VMEM((tok, a1.shape[1]), BF)],
    )


def gated_body(
    ids, p, q, bc0, bc1, got_s, got_v, got_w, state0, end_row, gain, wo,
    z, far_r, far_l, squares,
):
    carry0 = jnp.where(ids[4] > 0, 1.0, 0.0)
    carry1 = jnp.where(ids[5] > 0, 1.0, 0.0)
    sums = [None, None]
    for j in range(5):
        c = wide(j)
        more = got_s[128:, c].astype(F32)
        decay1 = more[0:1, :] + more[1:2, :] + more[2:3, :]
        more = got_v[128:, c].astype(F32)
        decay2 = more[0:1, :] + more[1:2, :] + more[2:3, :]
        entering = got_s[:128, c].astype(F32) + decay1 * (
            got_v[:128, c].astype(F32) + decay2 * got_w[:, c].astype(F32)
        )
        start0 = entering * carry0
        start1 = (end_row[0:1, c] * start0 + state0[:, c]) * carry1
        for block, start, bc in ((0, start0, bc0), (1, start1, bc1)):
            rows = block_rows(block)
            from_start = dot(bc[:, 128:], start.astype(BF))
            gated = p[rows, c] + q[rows, c] * from_start
            square = gated * gated
            square = square[:, :128] + square[:, 128:]
            sums[block] = square if sums[block] is None else sums[block] + square
            z[rows, c] = (gated * gain[0:1, c]).astype(BF)
    ncol = wo.shape[1] // RING
    top, low = block_rows(0), block_rows(1)
    far_r[:STRETCH, :] = dot(z[top, :], wo[:, chunk_of(ids, 3, ncol)]).astype(BF)
    far_l[:STRETCH, :] = dot(z[low, :], wo[:, chunk_of(ids, 3, ncol)]).astype(BF)
    row = lax.broadcasted_iota(jnp.int32, (16, STRETCH), 0)
    for block in range(2):
        c = block_rows(block)
        flat = jnp.sum(jnp.transpose(sums[block]), axis=0, keepdims=True)
        squares[:, c] = jnp.broadcast_to(flat, (8, STRETCH))
        packed = step_rows(row, flat).astype(BF)
        far_r[STRETCH:, c] = packed
        far_l[STRETCH:, c] = packed
    far_r[STRETCH:, 512:] = jnp.zeros((16, ncol - 512), BF)
    far_l[STRETCH:, 512:] = jnp.zeros((16, ncol - 512), BF)


def gated_part(ids, p, q, bc0, bc1, got_s, got_v, got_w, state0, end_row, gain, wo):
    tok, nv = p.shape
    ncol = wo.shape[1] // RING
    return call(
        gated_body,
        [
            shape((tok, nv), BF),
            shape((STRETCH + 16, ncol), BF),
            shape((STRETCH + 16, ncol), BF),
            shape((8, tok)),
        ],
        (ids, p, q, bc0, bc1, got_s, got_v, got_w, state0, end_row, gain, wo),
        "gated_part",
        2 * tok * nv * (ncol + 128),
    )


def near_body(ids, z, wo, far_r, far_l, dir_r, dir_l, top_r, low_l):
    ncol = wo.shape[1] // RING
    dir_r[...] = dot(z[STRETCH:, :], wo[:, chunk_of(ids, 2, ncol)]).astype(BF)
    dir_l[...] = dot(z[:STRETCH, :], wo[:, chunk_of(ids, 1, ncol)]).astype(BF)
    top_r[...] = dot(z[:STRETCH, :], wo[:, chunk_of(ids, 2, ncol)])
    low_l[...] = dot(z[STRETCH:, :], wo[:, chunk_of(ids, 1, ncol)])


def near_part(ids, z, wo, far_r, far_l):
    tok, nv = z.shape
    ncol = wo.shape[1] // RING
    outs = [shape((STRETCH, ncol), BF)] * 2 + [shape((STRETCH, ncol))] * 2
    return call(near_body, outs, (ids, z, wo, far_r, far_l), "near_part", 4 * tok * nv * ncol)


def mine_body(ids, z, wo, low_r, top_l, own):
    ncol = wo.shape[1] // RING
    at = chunk_of(ids, 0, ncol)
    own[:STRETCH, :] = dot(z[:STRETCH, :], wo[:, at]) + top_l[...].astype(F32)
    own[STRETCH:, :] = dot(z[STRETCH:, :], wo[:, at]) + low_r[...].astype(F32)


def mine_part(ids, z, wo, low_r, top_l):
    tok, nv = z.shape
    ncol = wo.shape[1] // RING
    return call(
        mine_body,
        [shape((tok, ncol))],
        (ids, z, wo, low_r, top_l),
        "mine_part",
        4 * tok * nv * ncol,
    )[0]


def add_body(ids, a1, b1, a2, b2, sent_r, sent_l, o1, o2):
    o1[:STRETCH, :] = (a1[...] + b1[:STRETCH, :].astype(F32)).astype(BF)
    o1[STRETCH:, :] = b1[STRETCH:, :]
    o2[...] = (a2[...] + b2[:STRETCH, :].astype(F32)).astype(BF)


def add_part(ids, a1, b1, a2, b2, sent_r, sent_l):
    return call(
        add_body,
        [shape(b1.shape, BF), shape(a2.shape, BF)],
        (ids, a1, b1, a2, b2, sent_r, sent_l),
        "add_part",
        2 * a1.size,
    )


def final_body(ids, own, top_r, low_l, mine, sq_r, sq_l, out):
    total = mine[0:1, :]
    for other in (sq_r, sq_l, top_r):
        more = other[STRETCH:, :512].astype(F32)
        total = total + (more[0:1, :] + more[1:2, :] + more[2:3, :])
    inv = lax.rsqrt(total * (1.0 / 5120.0) + 1e-05)
    inv = jnp.transpose(jnp.broadcast_to(inv, (128, inv.shape[1])))
    for block, got in ((0, top_r), (1, low_l)):
        rows = block_rows(block)
        scale = inv[rows, :]
        for low in range(0, out.shape[1], 128):
            c = slice(low, low + 128)
            out[rows, c] = ((own[rows, c] + got[:STRETCH, c].astype(F32)) * scale).astype(BF)


def final_part(ids, own, top_r, low_l, mine, sq_r, sq_l):
    return call(
        final_body,
        [shape(own.shape, BF)],
        (ids, own, top_r, low_l, mine, sq_r, sq_l),
        "final_part",
        4 * own.size,
    )[0]


def on_device(
    tokens,
    send_rows,
    send_counts,
    stretch_segments,
    main_proj,
    state_proj,
    step_proj,
    conv_main,
    conv_state,
    step_bias,
    decay_log,
    skip_gain,
    norm_gain,
    out_proj,
):
    ctx = lax.axis_index("ctx").astype(jnp.int32)
    head = lax.axis_index("head").astype(jnp.int32)
    tok, width = tokens.shape
    sources, slots = send_rows.shape[1:]
    heads = step_bias.shape[0]
    inner = main_proj.shape[2]
    head_dim = inner // heads

    send_list = send_rows.reshape(sources * slots)
    pick = (send_list[:, None] == jnp.arange(tok, dtype=jnp.int32)[None, :]).astype(BF)
    outgoing = dot(pick, tokens).astype(BF).reshape(sources, slots, width)
    arrived = lax.all_to_all(outgoing, "ctx", split_axis=0, concat_axis=0, tiled=True)

    blocks = tok // STRETCH
    block_ids = ctx * blocks + jnp.arange(blocks, dtype=jnp.int32)
    segment = jnp.take(stretch_segments, block_ids)
    before = jnp.take(stretch_segments, jnp.maximum(block_ids - 1, 0))
    carry = ((segment == before) & (block_ids > 0)).astype(jnp.int32)
    ring = jnp.stack([head, head + 3, head + 1, head + 2]) % RING
    ids = jnp.concatenate([ring, carry]).astype(jnp.int32)
    wm = flat_part(ids, main_proj)
    pad = ((0, 128 - heads),)
    head_rows = jnp.stack(
        [jnp.pad(step_bias, pad), jnp.pad(jnp.exp(decay_log), pad), jnp.pad(skip_gain, pad)]
    )
    head_rows = jnp.pad(head_rows, ((0, 5), (0, 0)))
    gain = norm_gain[None, :]

    column = jnp.take(send_counts, ctx, axis=1)
    begins = jnp.cumsum(column) - column
    slot = jnp.arange(slots, dtype=jnp.int32)[None, :]
    target = jnp.where(slot < column[:, None], begins[:, None] + slot, -1)
    target = target.reshape(1, sources * slots)
    arrived, wm, target, head_rows, gain, ids = lax.optimization_barrier(
        (arrived, wm, target, head_rows, gain, ids)
    )
    second, first, last = arrange_part(ids, target, arrived.reshape(sources * slots, width))
    weights = (state_proj, step_proj, wm)
    taps = (conv_state, conv_main, head_rows)

    r1 = turned(second, 1)
    l1 = turned(second, -1)
    t = shifted(last, 1)
    acc1 = own_part(ids, second, *weights)
    first = jnp.concatenate([t, first], axis=0)
    r1, l1, acc1, first = lax.optimization_barrier((r1, l1, acc1, first))
    cut = STRETCH // 2 + TAIL
    b1 = turned(r1[:cut], 1)
    b2 = turned(l1[cut:], -1)
    acc1 = next_part(ids, r1, l1, *weights, acc1)
    first, acc1 = lax.optimization_barrier((first, acc1))
    r0 = turned(first, 1)
    l0 = turned(first, -1)
    acc0 = own_part(ids, first, *weights)
    b1, b2, acc1, acc0 = lax.optimization_barrier((b1, b2, acc1, acc0))
    *block1, payload, mid, mid_step = second_part(ids, b1, b2, *weights, acc1, *taps)
    got_s = shifted(payload, 1)
    r0, l0, acc0, payload = lax.optimization_barrier((r0, l0, acc0, payload))
    cut = STRETCH // 2
    a1 = turned(r0[:cut], 1)
    a2 = turned(l0[cut:], -1)
    acc0 = next_part(ids, r0, l0, *weights, acc0)
    *block0, joined, joined_low, state0, end_row = first_part(
        ids, a1, a2, *weights, acc0, *taps, mid, mid_step, got_s
    )

    got_v = shifted(joined, 1)
    got_w = shifted(joined_low, 2)
    p, q = mix_part(ids, a1, a2, b1, b2, wm, acc0, acc1, head_rows, block0, block1)

    z, far_r, far_l, squares = gated_part(
        ids, p, q, block0[1], block1[1], got_s, got_v, got_w, state0, end_row, gain, out_proj
    )
    got_r = turned(far_r, 1)
    got_l = turned(far_l, -1)
    dir_r, dir_l, top_r, low_l = near_part(ids, z, out_proj, far_r, far_l)
    low_r = turned(dir_r, 1)
    top_l = turned(dir_l, -1)
    sum_r, sum_l = add_part(ids, top_r, got_r, low_l, got_l, dir_r, dir_l)
    top_r = turned(sum_r, 1)
    low_l = turned(sum_l, -1)
    own = mine_part(ids, z, out_proj, low_r, top_l)
    return final_part(ids, own, top_r, low_l, squares, got_r, got_l)


def solution(mesh):
    return jax.shard_map(
        on_device,
        mesh=mesh,
        in_specs=(
            P("ctx", "head"),
            P("ctx", None, None),
            P(),
            P(),
            P(None, None, "head"),
            P(),
            P(None, "head"),
            P(None, "head"),
            P(),
            P("head"),
            P("head"),
            P("head"),
            P("head"),
            P("head", None),
        ),
        out_specs=P("ctx", "head"),
        check_vma=False,
    )
```

```python
import jax
import jax.numpy as jnp
from jax import lax
from jax.experimental import pallas as pl
from jax.experimental.pallas import tpu as pltpu
from jax.sharding import PartitionSpec as P

BF = jnp.bfloat16
F32 = jnp.float32
STRETCH = 256
TAIL = 16
TILE = 256
LOG2E = 1.4426950408889634
RING = 4
VMEM = 16 * 1024 * 1024


def dot(a, b):
    return jnp.dot(a, b, preferred_element_type=F32)


def turned(value, steps):
    return lax.ppermute(value, "head", [(i, (i + steps) % RING) for i in range(RING)])


def shifted(value, steps):
    count = lax.axis_size("ctx")
    return lax.ppermute(value, "ctx", [(i, i + steps) for i in range(count - steps)])


def silu(v):
    return v * (1.0 / (1.0 + jnp.exp(-v)))


def split3(x):
    high = x.astype(BF).astype(F32)
    rest = x - high
    mid = rest.astype(BF).astype(F32)
    low = (rest - mid).astype(BF).astype(F32)
    return high, mid, low


def pack3(x):
    high, mid, low = split3(x)
    return (high + pltpu.roll(mid, 32, 1) + pltpu.roll(low, 64, 1)).astype(BF)


def spread(tile, width):
    lane = lax.broadcasted_iota(jnp.int32, (128, width), 0)
    col = lax.broadcasted_iota(jnp.int32, (128, width), 1)
    hit = ((lane & 31) == tile * (width // 64) + (col >> 6)) & (lane < 96)
    return jnp.where(hit, 1.0, 0.0).astype(BF)


def call(body, outs, args, name, flops, exps=0, scratch=()):
    size = sum(a.size * a.dtype.itemsize for a in args[1:]) + sum(
        o.size * o.dtype.itemsize for o in outs
    )
    return pl.pallas_call(
        body,
        in_specs=[pl.BlockSpec(memory_space=pltpu.SMEM)]
        + [pl.BlockSpec(memory_space=pltpu.VMEM)] * (len(args) - 1),
        out_specs=[pl.BlockSpec(memory_space=pltpu.VMEM)] * len(outs),
        out_shape=outs,
        scratch_shapes=scratch,
        compiler_params=pltpu.CompilerParams(vmem_limit_bytes=VMEM),
        cost_estimate=pl.CostEstimate(
            flops=int(flops), bytes_accessed=int(size), transcendentals=int(exps)
        ),
        name=name,
    )(*args)


def shape(dims, dtype=F32):
    return jax.ShapeDtypeStruct(dims, dtype)


def chunk_of(ids, at, k):
    return pl.ds(pl.multiple_of(ids[at] * k, 128), k)


def wide(j):
    return slice(j * TILE, (j + 1) * TILE)


def block_rows(block):
    return slice(block * STRETCH, (block + 1) * STRETCH)


def flat_body(ids, w, out):
    k = w.shape[0]
    for low in range(0, k, STRETCH):
        rows = slice(low, low + STRETCH)
        out[rows, :] = w[rows].reshape(STRETCH, out.shape[1])


def flat_part(ids, w):
    out = shape((w.shape[0], 2 * w.shape[2]), BF)
    return call(flat_body, [out], (ids, w), "flat_part", 1e9)[0]


CUT = STRETCH - TAIL


def arrange_body(ids, target, arrived, second, first, last):
    slots = arrived.shape[0]
    for low, high in ((CUT, 2 * STRETCH), (0, CUT)):
        row = lax.broadcasted_iota(jnp.int32, (high - low, slots), 0) + low
        pick = jnp.where(row == target[...], 1.0, 0.0).astype(BF)
        rows = dot(pick, arrived[...]).astype(BF)
        if low:
            second[...] = rows
            last[...] = rows[high - low - TAIL :, :]
        else:
            first[...] = rows


def arrange_part(ids, target, arrived):
    slots, k = arrived.shape
    return call(
        arrange_body,
        [shape((STRETCH + TAIL, k), BF), shape((CUT, k), BF), shape((TAIL, k), BF)],
        (ids, target, arrived),
        "arrange_part",
        2 * 512 * slots * k,
    )


def own_body(ids, x, sp, tp, wm, acc):
    at = chunk_of(ids, 0, x.shape[1])
    acc[:, 2560:2816] = dot(x[...], sp[at, :])
    acc[:, 2816 : 2816 + tp.shape[1]] = dot(x[...], tp[at, :])
    for j in range(10):
        acc[:, wide(j)] = dot(x[...], wm[at, wide(j)])


def own_part(ids, x, sp, tp, wm):
    rows, k = x.shape
    n = 2944
    return call(own_body, [shape((rows, n))], (ids, x, sp, tp, wm), "own_part", 2 * rows * k * n)[0]


def more_part(ids, x, which, sp, tp, wm, acc):
    rows, k = x.shape
    n = acc.shape[1]

    def body(ids, x, sp, tp, wm, before, acc):
        at = chunk_of(ids, which, k)
        c = slice(2560, 2816)
        acc[:, c] = before[:, c] + dot(x[...], sp[at, :])
        c = slice(2816, 2816 + tp.shape[1])
        acc[:, c] = before[:, c] + dot(x[...], tp[at, :])
        for j in range(10):
            c = wide(j)
            acc[:, c] = before[:, c] + dot(x[...], wm[at, c])

    return call(
        body, [shape((rows, n))], (ids, x, sp, tp, wm, acc), "more_part", 2 * rows * k * n
    )[0]


def three_body(ids, x, r, l, sp, tp, wm, acc):
    k = x.shape[1]
    pieces = [(p[...], chunk_of(ids, i, k)) for i, p in enumerate((x, r, l))]

    def project(w, c):
        return sum(dot(p, w[at, c]) for p, at in pieces)

    for j in range(10):
        acc[:, wide(j)] = project(wm, wide(j))
    acc[:, 2560:2816] = project(sp, slice(0, 256))
    acc[:, 2816 : 2816 + tp.shape[1]] = project(tp, slice(0, tp.shape[1]))


def three_part(ids, x, r, l, sp, tp, wm):
    rows, k = x.shape
    n = 2944
    return call(
        three_body, [shape((rows, n))], (ids, x, r, l, sp, tp, wm), "three_part", 6 * rows * k * n
    )[0]


def rounded(x):
    return x.astype(BF).astype(F32)


def conv_silu(xs, taps):
    total = None
    for k in range(4):
        term = xs[5 + k : 5 + k + STRETCH, :] * taps[k : k + 1, :]
        total = term if total is None else total + term
    return silu(total).astype(BF)


def step_rows(row, value):
    high, mid, low = split3(value)
    return jnp.where(row == 0, high, jnp.where(row == 1, mid, jnp.where(row == 2, low, 0.0)))


def decays(raw, heads, cum3, cum_t, step_t, ecum3):
    lane = lax.broadcasted_iota(jnp.int32, (STRETCH, 128), 1)
    row_id = lax.broadcasted_iota(jnp.int32, (STRETCH, STRETCH), 0)
    col_id = lax.broadcasted_iota(jnp.int32, (STRETCH, STRETCH), 1)
    below = jnp.where(row_id >= col_id, 1.0, 0.0).astype(BF)
    raw = jnp.where(lane < 20, raw, 0.0) + heads[0:1, :]
    small = jnp.exp(-jnp.abs(raw))
    one = 1.0 + small
    log_one = jnp.where(one == 1.0, small, jnp.log(one) * (small / (one - 1.0 + 1e-30)))
    step = jnp.where(lane < 20, jnp.maximum(raw, 0.0) + log_one, 0.0)
    sums = dot(below, pack3(step * (heads[1:2, :] * (-LOG2E))))
    sums = sums + pltpu.roll(sums, 96, 1) + pltpu.roll(sums, 64, 1)
    sums = jnp.where(lane < 32, sums, 0.0)
    final = sums[STRETCH - 1 : STRETCH, :]
    cum3[...] = pack3(sums)
    cum_t[...] = jnp.transpose(sums)[:32]
    step_t[...] = jnp.transpose(step)[:32]
    ecum3[...] = pack3(jnp.where(lane < 32, jnp.exp2(sums), 0.0))
    weights = pack3(jnp.exp2(final - sums) * step)
    ends = pack3(jnp.broadcast_to(jnp.where(lane[:1] < 32, jnp.exp2(final), 0.0), (16, 128)))
    return weights, ends


def second_body(
    ids, o1, o2, sp, tp, wm, acc, taps_s, taps_v, heads,
    act, bc, cum3, cum_t, step_t, ecum3, payload, mid, mid_step, xs,
):
    k = o1.shape[1]
    n1 = o1.shape[0]
    at = chunk_of(ids, 3, k)

    def channels(slot, c, w):
        buf = xs.at[slot]
        first = rounded(acc[:n1, c] + dot(o1[...], w))
        buf[8 : n1 - 8, :] = first[TAIL:, :]
        buf[:8, :] = jnp.where(ids[5] > 0, first[8:TAIL, :], 0.0)
        buf[n1 - 8 : STRETCH + 8, :] = rounded(acc[n1:, c] + dot(o2[...], w))
        return buf, first[:TAIL, :]

    buf, edge = channels(0, slice(2560, 2816), sp[at, :])
    mid[:, 1280:] = edge
    bc[...] = conv_silu(buf, taps_s)
    bt = jnp.transpose(bc[:, :128].astype(F32)).astype(BF)
    n = tp.shape[1]
    buf = xs.at[3]
    buf[:n1, :n] = acc[:n1, 2816 : 2816 + n] + dot(o1[...], tp[at, :])
    buf[n1:, :n] = acc[n1:, 2816 : 2816 + n] + dot(o2[...], tp[at, :])
    mid_step[...] = buf[:TAIL, :128]
    weights, ends = decays(buf[TAIL : TAIL + STRETCH, :128], heads, cum3, cum_t, step_t, ecum3)
    carry = jnp.where(ids[5] > 0, 1.0, 0.0)
    row = lax.broadcasted_iota(jnp.int32, (16, TILE), 0)
    for j in range(5):
        c = wide(j)
        buf, edge = channels(1 + j % 2, wide(5 + j), wm[at, wide(5 + j)])
        mid[:, c] = edge
        value = conv_silu(buf, taps_v[:, c])
        act[:, c] = value
        select = spread(j, TILE)
        weighted = (value.astype(F32) * dot(weights, select)).astype(BF)
        payload[:128, c] = dot(bt, weighted).astype(BF)
        payload[128:, c] = step_rows(row, dot(ends, select) * carry).astype(BF)


def block_outs():
    return [
        shape((STRETCH, 1280), BF),
        shape((STRETCH, 256), BF),
        shape((STRETCH, 128), BF),
        shape((32, STRETCH)),
        shape((32, STRETCH)),
        shape((STRETCH, 128), BF),
    ]


def second_part(ids, o1, o2, sp, tp, wm, acc, taps_s, taps_v, heads):
    return call(
        second_body,
        block_outs() + [shape((144, 1280), BF), shape((TAIL, 1536)), shape((TAIL, 128))],
        (ids, o1, o2, sp, tp, wm, acc, taps_s, taps_v, heads),
        "second_part",
        4 * STRETCH * 640 * 1664,
        scratch=[pltpu.VMEM((4, STRETCH + TAIL, TILE), F32)],
    )


def first_body(
    ids, o1, o2, sp, tp, wm, acc, taps_s, taps_v, heads, mid, mid_step, got,
    act, bc, cum3, cum_t, step_t, ecum3, joined, joined_low, state0, end_row, xs,
):
    k = o1.shape[1]
    n1 = o1.shape[0]
    at = chunk_of(ids, 3, k)

    def channels(slot, c, w, edge):
        buf = xs.at[slot]
        first = rounded(acc[:n1, c] + dot(o1[...], w))
        buf[8 : n1 - 8, :] = first[TAIL:, :]
        buf[:8, :] = jnp.where(ids[4] > 0, first[8:TAIL, :], 0.0)
        buf[n1 - 8 : STRETCH - 8, :] = rounded(acc[n1:, c] + dot(o2[...], w))
        buf[STRETCH - 8 : STRETCH + 8, :] = edge
        return buf

    buf = channels(0, slice(2560, 2816), sp[at, :], mid[:, 1280:])
    bc[...] = conv_silu(buf, taps_s)
    bt = jnp.transpose(bc[:, :128].astype(F32)).astype(BF)
    n = tp.shape[1]
    buf = xs.at[3]
    buf[:n1, :n] = acc[:n1, 2816 : 2816 + n] + dot(o1[...], tp[at, :])
    buf[n1:STRETCH, :n] = acc[n1:, 2816 : 2816 + n] + dot(o2[...], tp[at, :])
    buf[STRETCH:, :128] = mid_step[...]
    weights, ends = decays(buf[TAIL : TAIL + STRETCH, :128], heads, cum3, cum_t, step_t, ecum3)
    carry = jnp.where(ids[4] > 0, 1.0, 0.0)
    row = lax.broadcasted_iota(jnp.int32, (16, TILE), 0)
    for j in range(5):
        c = wide(j)
        buf = channels(1 + j % 2, wide(5 + j), wm[at, wide(5 + j)], mid[:, c])
        value = conv_silu(buf, taps_v[:, c])
        act[:, c] = value
        select = spread(j, TILE)
        weighted = (value.astype(F32) * dot(weights, select)).astype(BF)
        state = dot(bt, weighted)
        end = dot(ends, select)
        state0[:, c] = state
        end_row[:, c] = end[:8, :]
        decay = end[0:1, :] * carry
        more = got[128:, c].astype(F32)
        before = more[0:1, :] + more[1:2, :] + more[2:3, :]
        low = (state + decay * got[:128, c].astype(F32)).astype(BF)
        joined[:128, c] = low
        joined_low[:, c] = low
        joined[128:, c] = step_rows(row, decay * before).astype(BF)


def first_part(ids, o1, o2, sp, tp, wm, acc, taps_s, taps_v, heads, mid, mid_step, got):
    return call(
        first_body,
        block_outs()
        + [shape((144, 1280), BF), shape((128, 1280), BF), shape((128, 1280)), shape((8, 1280))],
        (ids, o1, o2, sp, tp, wm, acc, taps_s, taps_v, heads, mid, mid_step, got),
        "first_part",
        4 * STRETCH * 640 * 1664,
        scratch=[pltpu.VMEM((4, STRETCH + TAIL, TILE), F32)],
    )


def mix_body(
    ids, a1, a2, b1, b2, wm, acc0, acc1, heads,
    act0, bc0, cum30, cum_t0, step_t0, ecum30,
    act1, bc1, cum31, cum_t1, step_t1, ecum31,
    p_out, q_out, sc, xo,
):
    k = a1.shape[1]
    at = chunk_of(ids, 3, k)
    low = 0
    for piece in (a1[TAIL:, :], a2[...], b1[...], b2[...]):
        xo[low : low + piece.shape[0], :] = piece
        low += piece.shape[0]
    row_id = lax.broadcasted_iota(jnp.int32, (STRETCH, STRETCH), 0)
    col_id = lax.broadcasted_iota(jnp.int32, (STRETCH, STRETCH), 1)
    for block, bc in ((0, bc0), (1, bc1)):
        scores = lax.dot_general(
            bc[:, 128:], bc[:, :128], (((1,), (1,)), ((), ())), preferred_element_type=F32
        )
        sc[block] = jnp.where(row_id >= col_id, scores, 0.0)
    half = STRETCH // 2
    heads3 = pack3(heads[...])

    def one(i, _):
        c = pl.ds(pl.multiple_of(i * TILE, TILE), TILE)
        select = spread(i, TILE)
        skip = dot(heads3, select)[2:3, :]
        lane = lax.broadcasted_iota(jnp.int32, (128, STRETCH), 0)
        group = lax.broadcasted_iota(jnp.int32, (STRETCH, TILE), 1) >> 6
        for block, act, cum3, cum_t, step_t, ecum3 in (
            (1, act1, cum31, cum_t1, step_t1, ecum31),
            (0, act0, cum30, cum_t0, step_t0, ecum30),
        ):
            rows = block_rows(block)
            if block:
                gate = acc1[TAIL:, c]
            else:
                gate = jnp.concatenate([acc0[TAIL:, c], acc1[:TAIL, c]], axis=0)
            gate = silu(rounded(gate + dot(xo[rows, :], wm[at, c])))
            values = act[:, c]
            top = jnp.zeros((half, TILE), F32)
            bottom = jnp.zeros((half, TILE), F32)
            for j in range(TILE // 64):
                h = i * (TILE // 64) + j
                pick = jnp.where(((lane & 31) == h) & (lane < 96), 1.0, 0.0).astype(BF)
                cum = dot(cum3[...], pick)
                cum_s = cum_t[pl.ds(h, 1), :]
                step_s = step_t[pl.ds(h, 1), :]
                mine = jnp.where(group == j, values, jnp.zeros_like(values))
                m_top = (
                    sc[block, :half, :half]
                    * jnp.exp2(jnp.minimum(cum[:half, :half] - cum_s[:, :half], 0.0))
                    * step_s[:, :half]
                ).astype(BF)
                m_bottom = (
                    sc[block, half:, :]
                    * jnp.exp2(jnp.minimum(cum[half:, :] - cum_s, 0.0))
                    * step_s
                ).astype(BF)
                top = top + dot(m_top, mine[:half, :])
                bottom = bottom + dot(m_bottom, mine)
            within = jnp.concatenate([top, bottom], axis=0)
            p_out[rows, c] = (within + skip * values.astype(F32)) * gate
            q_out[rows, c] = dot(ecum3[...], select) * gate
        return 0

    lax.fori_loop(0, act0.shape[1] // TILE, one, 0)


def mix_part(ids, a1, a2, b1, b2, wm, acc0, acc1, heads, block0, block1):
    tok = 2 * STRETCH
    return call(
        mix_body,
        [shape((tok, 1280))] * 2,
        (ids, a1, a2, b1, b2, wm, acc0, acc1, heads, *block0, *block1),
        "mix_part",
        8e9,
        exps=20 * 512 * 256,
        scratch=[pltpu.VMEM((2, STRETCH, STRETCH), F32), pltpu.VMEM((tok, a1.shape[1]), BF)],
    )


def gated_body(
    ids, p, q, bc0, bc1, got_s, got_v, got_w, state0, end_row, gain, wo,
    z, far_r, far_l, squares,
):
    carry0 = jnp.where(ids[4] > 0, 1.0, 0.0)
    carry1 = jnp.where(ids[5] > 0, 1.0, 0.0)
    sums = [None, None]
    for j in range(5):
        c = wide(j)
        more = got_s[128:, c].astype(F32)
        decay1 = more[0:1, :] + more[1:2, :] + more[2:3, :]
        more = got_v[128:, c].astype(F32)
        decay2 = more[0:1, :] + more[1:2, :] + more[2:3, :]
        entering = got_s[:128, c].astype(F32) + decay1 * (
            got_v[:128, c].astype(F32) + decay2 * got_w[:, c].astype(F32)
        )
        start0 = entering * carry0
        start1 = (end_row[0:1, c] * start0 + state0[:, c]) * carry1
        for block, start, bc in ((0, start0, bc0), (1, start1, bc1)):
            rows = block_rows(block)
            from_start = dot(bc[:, 128:], start.astype(BF))
            gated = p[rows, c] + q[rows, c] * from_start
            square = gated * gated
            square = square[:, :128] + square[:, 128:]
            sums[block] = square if sums[block] is None else sums[block] + square
            z[rows, c] = (gated * gain[0:1, c]).astype(BF)
    ncol = wo.shape[1] // RING
    top, low = block_rows(0), block_rows(1)
    far_r[:STRETCH, :] = dot(z[top, :], wo[:, chunk_of(ids, 3, ncol)]).astype(BF)
    far_l[:STRETCH, :] = dot(z[low, :], wo[:, chunk_of(ids, 3, ncol)]).astype(BF)
    row = lax.broadcasted_iota(jnp.int32, (16, STRETCH), 0)
    for block in range(2):
        c = block_rows(block)
        flat = jnp.sum(jnp.transpose(sums[block]), axis=0, keepdims=True)
        squares[:, c] = jnp.broadcast_to(flat, (8, STRETCH))
        packed = step_rows(row, flat).astype(BF)
        far_r[STRETCH:, c] = packed
        far_l[STRETCH:, c] = packed
    far_r[STRETCH:, 512:] = jnp.zeros((16, ncol - 512), BF)
    far_l[STRETCH:, 512:] = jnp.zeros((16, ncol - 512), BF)


def gated_part(ids, p, q, bc0, bc1, got_s, got_v, got_w, state0, end_row, gain, wo):
    tok, nv = p.shape
    ncol = wo.shape[1] // RING
    return call(
        gated_body,
        [
            shape((tok, nv), BF),
            shape((STRETCH + 16, ncol), BF),
            shape((STRETCH + 16, ncol), BF),
            shape((8, tok)),
        ],
        (ids, p, q, bc0, bc1, got_s, got_v, got_w, state0, end_row, gain, wo),
        "gated_part",
        2 * tok * nv * (ncol + 128),
    )


def near_body(ids, z, wo, far_r, far_l, dir_r, dir_l, top_r, low_l):
    ncol = wo.shape[1] // RING
    dir_r[...] = dot(z[STRETCH:, :], wo[:, chunk_of(ids, 2, ncol)]).astype(BF)
    dir_l[...] = dot(z[:STRETCH, :], wo[:, chunk_of(ids, 1, ncol)]).astype(BF)
    top_r[...] = dot(z[:STRETCH, :], wo[:, chunk_of(ids, 2, ncol)])
    low_l[...] = dot(z[STRETCH:, :], wo[:, chunk_of(ids, 1, ncol)])


def near_part(ids, z, wo, far_r, far_l):
    tok, nv = z.shape
    ncol = wo.shape[1] // RING
    outs = [shape((STRETCH, ncol), BF)] * 2 + [shape((STRETCH, ncol))] * 2
    return call(near_body, outs, (ids, z, wo, far_r, far_l), "near_part", 4 * tok * nv * ncol)


def mine_body(ids, z, wo, low_r, top_l, own):
    ncol = wo.shape[1] // RING
    at = chunk_of(ids, 0, ncol)
    own[:STRETCH, :] = dot(z[:STRETCH, :], wo[:, at]) + top_l[...].astype(F32)
    own[STRETCH:, :] = dot(z[STRETCH:, :], wo[:, at]) + low_r[...].astype(F32)


def mine_part(ids, z, wo, low_r, top_l):
    tok, nv = z.shape
    ncol = wo.shape[1] // RING
    return call(
        mine_body,
        [shape((tok, ncol))],
        (ids, z, wo, low_r, top_l),
        "mine_part",
        4 * tok * nv * ncol,
    )[0]


def add_body(ids, a1, b1, a2, b2, sent_r, sent_l, o1, o2):
    o1[:STRETCH, :] = (a1[...] + b1[:STRETCH, :].astype(F32)).astype(BF)
    o1[STRETCH:, :] = b1[STRETCH:, :]
    o2[...] = (a2[...] + b2[:STRETCH, :].astype(F32)).astype(BF)


def add_part(ids, a1, b1, a2, b2, sent_r, sent_l):
    return call(
        add_body,
        [shape(b1.shape, BF), shape(a2.shape, BF)],
        (ids, a1, b1, a2, b2, sent_r, sent_l),
        "add_part",
        2 * a1.size,
    )


def final_body(ids, own, top_r, low_l, mine, sq_r, sq_l, out):
    total = mine[0:1, :]
    for other in (sq_r, sq_l, top_r):
        more = other[STRETCH:, :512].astype(F32)
        total = total + (more[0:1, :] + more[1:2, :] + more[2:3, :])
    inv = lax.rsqrt(total * (1.0 / 5120.0) + 1e-05)
    inv = jnp.transpose(jnp.broadcast_to(inv, (128, inv.shape[1])))
    for block, got in ((0, top_r), (1, low_l)):
        rows = block_rows(block)
        scale = inv[rows, :]
        for low in range(0, out.shape[1], 128):
            c = slice(low, low + 128)
            out[rows, c] = ((own[rows, c] + got[:STRETCH, c].astype(F32)) * scale).astype(BF)


def final_part(ids, own, top_r, low_l, mine, sq_r, sq_l):
    return call(
        final_body,
        [shape(own.shape, BF)],
        (ids, own, top_r, low_l, mine, sq_r, sq_l),
        "final_part",
        4 * own.size,
    )[0]


def on_device(
    tokens,
    send_rows,
    send_counts,
    stretch_segments,
    main_proj,
    state_proj,
    step_proj,
    conv_main,
    conv_state,
    step_bias,
    decay_log,
    skip_gain,
    norm_gain,
    out_proj,
):
    ctx = lax.axis_index("ctx").astype(jnp.int32)
    head = lax.axis_index("head").astype(jnp.int32)
    tok, width = tokens.shape
    sources, slots = send_rows.shape[1:]
    heads = step_bias.shape[0]
    inner = main_proj.shape[2]
    head_dim = inner // heads

    send_list = send_rows.reshape(sources * slots)
    pick = (send_list[:, None] == jnp.arange(tok, dtype=jnp.int32)[None, :]).astype(BF)
    outgoing = dot(pick, tokens).astype(BF).reshape(sources, slots, width)
    arrived = lax.all_to_all(outgoing, "ctx", split_axis=0, concat_axis=0, tiled=True)

    blocks = tok // STRETCH
    block_ids = ctx * blocks + jnp.arange(blocks, dtype=jnp.int32)
    segment = jnp.take(stretch_segments, block_ids)
    before = jnp.take(stretch_segments, jnp.maximum(block_ids - 1, 0))
    carry = ((segment == before) & (block_ids > 0)).astype(jnp.int32)
    ring = jnp.stack([head, head + 3, head + 1, head + 2]) % RING
    ids = jnp.concatenate([ring, carry]).astype(jnp.int32)
    wm = flat_part(ids, main_proj)
    pad = ((0, 128 - heads),)
    head_rows = jnp.stack(
        [jnp.pad(step_bias, pad), jnp.pad(jnp.exp(decay_log), pad), jnp.pad(skip_gain, pad)]
    )
    head_rows = jnp.pad(head_rows, ((0, 5), (0, 0)))
    gain = norm_gain[None, :]

    column = jnp.take(send_counts, ctx, axis=1)
    begins = jnp.cumsum(column) - column
    slot = jnp.arange(slots, dtype=jnp.int32)[None, :]
    target = jnp.where(slot < column[:, None], begins[:, None] + slot, -1)
    target = target.reshape(1, sources * slots)
    arrived, wm, target, head_rows, gain, ids = lax.optimization_barrier(
        (arrived, wm, target, head_rows, gain, ids)
    )
    second, first, last = arrange_part(ids, target, arrived.reshape(sources * slots, width))
    weights = (state_proj, step_proj, wm)
    taps = (conv_state, conv_main, head_rows)

    r1 = turned(second, 1)
    l1 = turned(second, -1)
    t = shifted(last, 1)
    acc1 = own_part(ids, second, *weights)
    first = jnp.concatenate([t, first], axis=0)
    r1, l1, acc1, first = lax.optimization_barrier((r1, l1, acc1, first))
    cut = STRETCH // 2 + TAIL
    b1 = turned(r1[:cut], 1)
    b2 = turned(l1[cut:], -1)
    acc1 = more_part(ids, r1, 1, *weights, acc1)
    first, acc1 = lax.optimization_barrier((first, acc1))
    r0 = turned(first, 1)
    l0 = turned(first, -1)
    acc1 = more_part(ids, l1, 2, *weights, acc1)
    b1, b2, acc1 = lax.optimization_barrier((b1, b2, acc1))
    *block1, payload, mid, mid_step = second_part(ids, b1, b2, *weights, acc1, *taps)
    got_s = shifted(payload, 1)
    r0, l0, payload = lax.optimization_barrier((r0, l0, payload))
    cut = STRETCH // 2
    a1 = turned(r0[:cut], 1)
    a2 = turned(l0[cut:], -1)
    acc0 = three_part(ids, first, r0, l0, *weights)
    *block0, joined, joined_low, state0, end_row = first_part(
        ids, a1, a2, *weights, acc0, *taps, mid, mid_step, got_s
    )

    got_v = shifted(joined, 1)
    got_w = shifted(joined_low, 2)
    p, q = mix_part(ids, a1, a2, b1, b2, wm, acc0, acc1, head_rows, block0, block1)

    z, far_r, far_l, squares = gated_part(
        ids, p, q, block0[1], block1[1], got_s, got_v, got_w, state0, end_row, gain, out_proj
    )
    got_r = turned(far_r, 1)
    got_l = turned(far_l, -1)
    dir_r, dir_l, top_r, low_l = near_part(ids, z, out_proj, far_r, far_l)
    low_r = turned(dir_r, 1)
    top_l = turned(dir_l, -1)
    sum_r, sum_l = add_part(ids, top_r, got_r, low_l, got_l, dir_r, dir_l)
    top_r = turned(sum_r, 1)
    low_l = turned(sum_l, -1)
    own = mine_part(ids, z, out_proj, low_r, top_l)
    return final_part(ids, own, top_r, low_l, squares, got_r, got_l)


def solution(mesh):
    return jax.shard_map(
        on_device,
        mesh=mesh,
        in_specs=(
            P("ctx", "head"),
            P("ctx", None, None),
            P(),
            P(),
            P(None, None, "head"),
            P(),
            P(None, "head"),
            P(None, "head"),
            P(),
            P("head"),
            P("head"),
            P("head"),
            P("head"),
            P("head", None),
        ),
        out_specs=P("ctx", "head"),
        check_vma=False,
    )
```

```python
import jax
import jax.numpy as jnp
from jax import lax
from jax.experimental import pallas as pl
from jax.experimental.pallas import tpu as pltpu
from jax.sharding import PartitionSpec as P

BF = jnp.bfloat16
F32 = jnp.float32
STRETCH = 256
TAIL = 16
TILE = 256
LOG2E = 1.4426950408889634
RING = 4
VMEM = 16 * 1024 * 1024


def dot(a, b):
    return jnp.dot(a, b, preferred_element_type=F32)


def turned(value, steps):
    return lax.ppermute(value, "head", [(i, (i + steps) % RING) for i in range(RING)])


def shifted(value, steps):
    count = lax.axis_size("ctx")
    return lax.ppermute(value, "ctx", [(i, i + steps) for i in range(count - steps)])


def silu(v):
    return v * (1.0 / (1.0 + jnp.exp(-v)))


def split3(x):
    high = x.astype(BF).astype(F32)
    rest = x - high
    mid = rest.astype(BF).astype(F32)
    low = (rest - mid).astype(BF).astype(F32)
    return high, mid, low


def pack3(x):
    high, mid, low = split3(x)
    return (high + pltpu.roll(mid, 32, 1) + pltpu.roll(low, 64, 1)).astype(BF)


def spread(tile, width):
    lane = lax.broadcasted_iota(jnp.int32, (128, width), 0)
    col = lax.broadcasted_iota(jnp.int32, (128, width), 1)
    hit = ((lane & 31) == tile * (width // 64) + (col >> 6)) & (lane < 96)
    return jnp.where(hit, 1.0, 0.0).astype(BF)


def call(body, outs, args, name, flops, exps=0, scratch=()):
    size = sum(a.size * a.dtype.itemsize for a in args[1:]) + sum(
        o.size * o.dtype.itemsize for o in outs
    )
    return pl.pallas_call(
        body,
        in_specs=[pl.BlockSpec(memory_space=pltpu.SMEM)]
        + [pl.BlockSpec(memory_space=pltpu.VMEM)] * (len(args) - 1),
        out_specs=[pl.BlockSpec(memory_space=pltpu.VMEM)] * len(outs),
        out_shape=outs,
        scratch_shapes=scratch,
        compiler_params=pltpu.CompilerParams(vmem_limit_bytes=VMEM),
        cost_estimate=pl.CostEstimate(
            flops=int(flops), bytes_accessed=int(size), transcendentals=int(exps)
        ),
        name=name,
    )(*args)


def shape(dims, dtype=F32):
    return jax.ShapeDtypeStruct(dims, dtype)


def chunk_of(ids, at, k):
    return pl.ds(pl.multiple_of(ids[at] * k, 128), k)


def wide(j):
    return slice(j * TILE, (j + 1) * TILE)


def block_rows(block):
    return slice(block * STRETCH, (block + 1) * STRETCH)


def flat_body(ids, w, out):
    k = w.shape[0]
    for low in range(0, k, STRETCH):
        rows = slice(low, low + STRETCH)
        out[rows, :] = w[rows].reshape(STRETCH, out.shape[1])


def flat_part(ids, w):
    out = shape((w.shape[0], 2 * w.shape[2]), BF)
    return call(flat_body, [out], (ids, w), "flat_part", 1e9)[0]


CUT = STRETCH - TAIL


def arrange_body(ids, target, arrived, second, first, last):
    slots = arrived.shape[0]
    for low, high in ((CUT, 2 * STRETCH), (0, CUT)):
        row = lax.broadcasted_iota(jnp.int32, (high - low, slots), 0) + low
        pick = jnp.where(row == target[...], 1.0, 0.0).astype(BF)
        rows = dot(pick, arrived[...]).astype(BF)
        if low:
            second[...] = rows
            last[...] = rows[high - low - TAIL :, :]
        else:
            first[...] = rows


def arrange_part(ids, target, arrived):
    slots, k = arrived.shape
    return call(
        arrange_body,
        [shape((STRETCH + TAIL, k), BF), shape((CUT, k), BF), shape((TAIL, k), BF)],
        (ids, target, arrived),
        "arrange_part",
        2 * 512 * slots * k,
    )


def own_body(ids, x, sp, tp, wm, acc):
    at = chunk_of(ids, 0, x.shape[1])
    acc[:, 2560:2816] = dot(x[...], sp[at, :])
    acc[:, 2816 : 2816 + tp.shape[1]] = dot(x[...], tp[at, :])
    for j in range(10):
        acc[:, wide(j)] = dot(x[...], wm[at, wide(j)])


def own_part(ids, x, sp, tp, wm):
    rows, k = x.shape
    n = 2944
    return call(own_body, [shape((rows, n))], (ids, x, sp, tp, wm), "own_part", 2 * rows * k * n)[0]


def next_body(ids, r, l, sp, tp, wm, before, acc):
    k = r.shape[1]
    at_r, at_l = chunk_of(ids, 1, k), chunk_of(ids, 2, k)
    c = slice(2560, 2816)
    acc[:, c] = before[:, c] + dot(r[...], sp[at_r, :]) + dot(l[...], sp[at_l, :])
    c = slice(2816, 2816 + tp.shape[1])
    acc[:, c] = before[:, c] + dot(r[...], tp[at_r, :]) + dot(l[...], tp[at_l, :])
    for j in range(10):
        c = wide(j)
        acc[:, c] = before[:, c] + dot(r[...], wm[at_r, c]) + dot(l[...], wm[at_l, c])


def next_part(ids, r, l, sp, tp, wm, acc):
    rows, k = r.shape
    n = acc.shape[1]
    return call(
        next_body, [shape((rows, n))], (ids, r, l, sp, tp, wm, acc), "next_part", 4 * rows * k * n
    )[0]


def rounded(x):
    return x.astype(BF).astype(F32)


def conv_silu(xs, taps):
    total = None
    for k in range(4):
        term = xs[5 + k : 5 + k + STRETCH, :] * taps[k : k + 1, :]
        total = term if total is None else total + term
    return silu(total).astype(BF)


def step_rows(row, value):
    high, mid, low = split3(value)
    return jnp.where(row == 0, high, jnp.where(row == 1, mid, jnp.where(row == 2, low, 0.0)))


def decays(raw, heads, cum3, cum_t, step_t, ecum3):
    lane = lax.broadcasted_iota(jnp.int32, (STRETCH, 128), 1)
    row_id = lax.broadcasted_iota(jnp.int32, (STRETCH, STRETCH), 0)
    col_id = lax.broadcasted_iota(jnp.int32, (STRETCH, STRETCH), 1)
    below = jnp.where(row_id >= col_id, 1.0, 0.0).astype(BF)
    raw = jnp.where(lane < 20, raw, 0.0) + heads[0:1, :]
    small = jnp.exp(-jnp.abs(raw))
    one = 1.0 + small
    log_one = jnp.where(one == 1.0, small, jnp.log(one) * (small / (one - 1.0 + 1e-30)))
    step = jnp.where(lane < 20, jnp.maximum(raw, 0.0) + log_one, 0.0)
    sums = dot(below, pack3(step * (heads[1:2, :] * (-LOG2E))))
    sums = sums + pltpu.roll(sums, 96, 1) + pltpu.roll(sums, 64, 1)
    sums = jnp.where(lane < 32, sums, 0.0)
    final = sums[STRETCH - 1 : STRETCH, :]
    cum3[...] = pack3(sums)
    cum_t[...] = jnp.transpose(sums)[:32]
    step_t[...] = jnp.transpose(step)[:32]
    ecum3[...] = pack3(jnp.where(lane < 32, jnp.exp2(sums), 0.0))
    weights = pack3(jnp.exp2(final - sums) * step)
    ends = pack3(jnp.broadcast_to(jnp.where(lane[:1] < 32, jnp.exp2(final), 0.0), (16, 128)))
    return weights, ends


def second_body(
    ids, o1, o2, sp, tp, wm, acc, taps_s, taps_v, heads,
    act, bc, cum3, cum_t, step_t, ecum3, payload, mid, mid_step, xs,
):
    k = o1.shape[1]
    n1 = o1.shape[0]
    at = chunk_of(ids, 3, k)

    def channels(slot, c, w):
        buf = xs.at[slot]
        first = rounded(acc[:n1, c] + dot(o1[...], w))
        buf[8 : n1 - 8, :] = first[TAIL:, :]
        buf[:8, :] = jnp.where(ids[5] > 0, first[8:TAIL, :], 0.0)
        buf[n1 - 8 : STRETCH + 8, :] = rounded(acc[n1:, c] + dot(o2[...], w))
        return buf, first[:TAIL, :]

    buf, edge = channels(0, slice(2560, 2816), sp[at, :])
    mid[:, 1280:] = edge
    bc[...] = conv_silu(buf, taps_s)
    bt = jnp.transpose(bc[:, :128].astype(F32)).astype(BF)
    n = tp.shape[1]
    buf = xs.at[3]
    buf[:n1, :n] = acc[:n1, 2816 : 2816 + n] + dot(o1[...], tp[at, :])
    buf[n1:, :n] = acc[n1:, 2816 : 2816 + n] + dot(o2[...], tp[at, :])
    mid_step[...] = buf[:TAIL, :128]
    weights, ends = decays(buf[TAIL : TAIL + STRETCH, :128], heads, cum3, cum_t, step_t, ecum3)
    carry = jnp.where(ids[5] > 0, 1.0, 0.0)
    row = lax.broadcasted_iota(jnp.int32, (16, TILE), 0)
    for j in range(5):
        c = wide(j)
        buf, edge = channels(1 + j % 2, wide(5 + j), wm[at, wide(5 + j)])
        mid[:, c] = edge
        value = conv_silu(buf, taps_v[:, c])
        act[:, c] = value
        select = spread(j, TILE)
        weighted = (value.astype(F32) * dot(weights, select)).astype(BF)
        payload[:128, c] = dot(bt, weighted).astype(BF)
        payload[128:, c] = step_rows(row, dot(ends, select) * carry).astype(BF)


def block_outs():
    return [
        shape((STRETCH, 1280), BF),
        shape((STRETCH, 256), BF),
        shape((STRETCH, 128), BF),
        shape((32, STRETCH)),
        shape((32, STRETCH)),
        shape((STRETCH, 128), BF),
    ]


def second_part(ids, o1, o2, sp, tp, wm, acc, taps_s, taps_v, heads):
    return call(
        second_body,
        block_outs() + [shape((144, 1280), BF), shape((TAIL, 1536)), shape((TAIL, 128))],
        (ids, o1, o2, sp, tp, wm, acc, taps_s, taps_v, heads),
        "second_part",
        4 * STRETCH * 640 * 1664,
        scratch=[pltpu.VMEM((4, STRETCH + TAIL, TILE), F32)],
    )


def first_body(
    ids, o1, o2, sp, tp, wm, acc, taps_s, taps_v, heads, mid, mid_step, got,
    act, bc, cum3, cum_t, step_t, ecum3, joined, joined_low, state0, end_row, xs,
):
    k = o1.shape[1]
    n1 = o1.shape[0]
    at = chunk_of(ids, 3, k)

    def channels(slot, c, w, edge):
        buf = xs.at[slot]
        first = rounded(acc[:n1, c] + dot(o1[...], w))
        buf[8 : n1 - 8, :] = first[TAIL:, :]
        buf[:8, :] = jnp.where(ids[4] > 0, first[8:TAIL, :], 0.0)
        buf[n1 - 8 : STRETCH - 8, :] = rounded(acc[n1:, c] + dot(o2[...], w))
        buf[STRETCH - 8 : STRETCH + 8, :] = edge
        return buf

    buf = channels(0, slice(2560, 2816), sp[at, :], mid[:, 1280:])
    bc[...] = conv_silu(buf, taps_s)
    bt = jnp.transpose(bc[:, :128].astype(F32)).astype(BF)
    n = tp.shape[1]
    buf = xs.at[3]
    buf[:n1, :n] = acc[:n1, 2816 : 2816 + n] + dot(o1[...], tp[at, :])
    buf[n1:STRETCH, :n] = acc[n1:, 2816 : 2816 + n] + dot(o2[...], tp[at, :])
    buf[STRETCH:, :128] = mid_step[...]
    weights, ends = decays(buf[TAIL : TAIL + STRETCH, :128], heads, cum3, cum_t, step_t, ecum3)
    carry = jnp.where(ids[4] > 0, 1.0, 0.0)
    row = lax.broadcasted_iota(jnp.int32, (16, TILE), 0)
    for j in range(5):
        c = wide(j)
        buf = channels(1 + j % 2, wide(5 + j), wm[at, wide(5 + j)], mid[:, c])
        value = conv_silu(buf, taps_v[:, c])
        act[:, c] = value
        select = spread(j, TILE)
        weighted = (value.astype(F32) * dot(weights, select)).astype(BF)
        state = dot(bt, weighted)
        end = dot(ends, select)
        state0[:, c] = state
        end_row[:, c] = end[:8, :]
        decay = end[0:1, :] * carry
        more = got[128:, c].astype(F32)
        before = more[0:1, :] + more[1:2, :] + more[2:3, :]
        low = (state + decay * got[:128, c].astype(F32)).astype(BF)
        joined[:128, c] = low
        joined_low[:, c] = low
        joined[128:, c] = step_rows(row, decay * before).astype(BF)


def first_part(ids, o1, o2, sp, tp, wm, acc, taps_s, taps_v, heads, mid, mid_step, got):
    return call(
        first_body,
        block_outs()
        + [shape((144, 1280), BF), shape((128, 1280), BF), shape((128, 1280)), shape((8, 1280))],
        (ids, o1, o2, sp, tp, wm, acc, taps_s, taps_v, heads, mid, mid_step, got),
        "first_part",
        4 * STRETCH * 640 * 1664,
        scratch=[pltpu.VMEM((4, STRETCH + TAIL, TILE), F32)],
    )


def mix_body(
    ids, a1, a2, b1, b2, wm, acc0, acc1, heads,
    act0, bc0, cum30, cum_t0, step_t0, ecum30,
    act1, bc1, cum31, cum_t1, step_t1, ecum31,
    p_out, q_out, sc, xo,
):
    k = a1.shape[1]
    at = chunk_of(ids, 3, k)
    low = 0
    for piece in (a1[TAIL:, :], a2[...], b1[...], b2[...]):
        xo[low : low + piece.shape[0], :] = piece
        low += piece.shape[0]
    row_id = lax.broadcasted_iota(jnp.int32, (STRETCH, STRETCH), 0)
    col_id = lax.broadcasted_iota(jnp.int32, (STRETCH, STRETCH), 1)
    for block, bc in ((0, bc0), (1, bc1)):
        scores = lax.dot_general(
            bc[:, 128:], bc[:, :128], (((1,), (1,)), ((), ())), preferred_element_type=F32
        )
        sc[block] = jnp.where(row_id >= col_id, scores, 0.0)
    half = STRETCH // 2
    heads3 = pack3(heads[...])

    def one(i, _):
        c = pl.ds(pl.multiple_of(i * TILE, TILE), TILE)
        select = spread(i, TILE)
        skip = dot(heads3, select)[2:3, :]
        lane = lax.broadcasted_iota(jnp.int32, (128, STRETCH), 0)
        group = lax.broadcasted_iota(jnp.int32, (STRETCH, TILE), 1) >> 6
        for block, act, cum3, cum_t, step_t, ecum3 in (
            (1, act1, cum31, cum_t1, step_t1, ecum31),
            (0, act0, cum30, cum_t0, step_t0, ecum30),
        ):
            rows = block_rows(block)
            if block:
                gate = acc1[TAIL:, c]
            else:
                gate = jnp.concatenate([acc0[TAIL:, c], acc1[:TAIL, c]], axis=0)
            gate = silu(rounded(gate + dot(xo[rows, :], wm[at, c])))
            values = act[:, c]
            top = jnp.zeros((half, TILE), F32)
            bottom = jnp.zeros((half, TILE), F32)
            for j in range(TILE // 64):
                h = i * (TILE // 64) + j
                pick = jnp.where(((lane & 31) == h) & (lane < 96), 1.0, 0.0).astype(BF)
                cum = dot(cum3[...], pick)
                cum_s = cum_t[pl.ds(h, 1), :]
                step_s = step_t[pl.ds(h, 1), :]
                mine = jnp.where(group == j, values, jnp.zeros_like(values))
                m_top = (
                    sc[block, :half, :half]
                    * jnp.exp2(jnp.minimum(cum[:half, :half] - cum_s[:, :half], 0.0))
                    * step_s[:, :half]
                ).astype(BF)
                m_bottom = (
                    sc[block, half:, :]
                    * jnp.exp2(jnp.minimum(cum[half:, :] - cum_s, 0.0))
                    * step_s
                ).astype(BF)
                top = top + dot(m_top, mine[:half, :])
                bottom = bottom + dot(m_bottom, mine)
            within = jnp.concatenate([top, bottom], axis=0)
            p_out[rows, c] = (within + skip * values.astype(F32)) * gate
            q_out[rows, c] = dot(ecum3[...], select) * gate
        return 0

    lax.fori_loop(0, act0.shape[1] // TILE, one, 0)


def mix_part(ids, a1, a2, b1, b2, wm, acc0, acc1, heads, block0, block1):
    tok = 2 * STRETCH
    return call(
        mix_body,
        [shape((tok, 1280))] * 2,
        (ids, a1, a2, b1, b2, wm, acc0, acc1, heads, *block0, *block1),
        "mix_part",
        8e9,
        exps=20 * 512 * 256,
        scratch=[pltpu.VMEM((2, STRETCH, STRETCH), F32), pltpu.VMEM((tok, a1.shape[1]), BF)],
    )


def gated_body(
    ids, p, q, bc0, bc1, got_s, got_v, got_w, state0, end_row, gain, wo,
    z, far_r, far_l, squares,
):
    carry0 = jnp.where(ids[4] > 0, 1.0, 0.0)
    carry1 = jnp.where(ids[5] > 0, 1.0, 0.0)
    sums = [None, None]
    for j in range(5):
        c = wide(j)
        more = got_s[128:, c].astype(F32)
        decay1 = more[0:1, :] + more[1:2, :] + more[2:3, :]
        more = got_v[128:, c].astype(F32)
        decay2 = more[0:1, :] + more[1:2, :] + more[2:3, :]
        entering = got_s[:128, c].astype(F32) + decay1 * (
            got_v[:128, c].astype(F32) + decay2 * got_w[:, c].astype(F32)
        )
        start0 = entering * carry0
        start1 = (end_row[0:1, c] * start0 + state0[:, c]) * carry1
        for block, start, bc in ((0, start0, bc0), (1, start1, bc1)):
            rows = block_rows(block)
            from_start = dot(bc[:, 128:], start.astype(BF))
            gated = p[rows, c] + q[rows, c] * from_start
            square = gated * gated
            square = square[:, :128] + square[:, 128:]
            sums[block] = square if sums[block] is None else sums[block] + square
            z[rows, c] = (gated * gain[0:1, c]).astype(BF)
    ncol = wo.shape[1] // RING
    top, low = block_rows(0), block_rows(1)
    far_r[:STRETCH, :] = dot(z[top, :], wo[:, chunk_of(ids, 3, ncol)]).astype(BF)
    far_l[:STRETCH, :] = dot(z[low, :], wo[:, chunk_of(ids, 3, ncol)]).astype(BF)
    row = lax.broadcasted_iota(jnp.int32, (16, STRETCH), 0)
    for block in range(2):
        c = block_rows(block)
        flat = jnp.sum(jnp.transpose(sums[block]), axis=0, keepdims=True)
        squares[:, c] = jnp.broadcast_to(flat, (8, STRETCH))
        packed = step_rows(row, flat).astype(BF)
        far_r[STRETCH:, c] = packed
        far_l[STRETCH:, c] = packed
    far_r[STRETCH:, 512:] = jnp.zeros((16, ncol - 512), BF)
    far_l[STRETCH:, 512:] = jnp.zeros((16, ncol - 512), BF)


def gated_part(ids, p, q, bc0, bc1, got_s, got_v, got_w, state0, end_row, gain, wo):
    tok, nv = p.shape
    ncol = wo.shape[1] // RING
    return call(
        gated_body,
        [
            shape((tok, nv), BF),
            shape((STRETCH + 16, ncol), BF),
            shape((STRETCH + 16, ncol), BF),
            shape((8, tok)),
        ],
        (ids, p, q, bc0, bc1, got_s, got_v, got_w, state0, end_row, gain, wo),
        "gated_part",
        2 * tok * nv * (ncol + 128),
    )


def near_body(ids, z, wo, far_r, far_l, dir_r, dir_l, top_r, low_l):
    ncol = wo.shape[1] // RING
    dir_r[...] = dot(z[STRETCH:, :], wo[:, chunk_of(ids, 2, ncol)]).astype(BF)
    dir_l[...] = dot(z[:STRETCH, :], wo[:, chunk_of(ids, 1, ncol)]).astype(BF)
    top_r[...] = dot(z[:STRETCH, :], wo[:, chunk_of(ids, 2, ncol)])
    low_l[...] = dot(z[STRETCH:, :], wo[:, chunk_of(ids, 1, ncol)])


def near_part(ids, z, wo, far_r, far_l):
    tok, nv = z.shape
    ncol = wo.shape[1] // RING
    outs = [shape((STRETCH, ncol), BF)] * 2 + [shape((STRETCH, ncol))] * 2
    return call(near_body, outs, (ids, z, wo, far_r, far_l), "near_part", 4 * tok * nv * ncol)


def mine_body(ids, z, wo, low_r, top_l, own):
    ncol = wo.shape[1] // RING
    at = chunk_of(ids, 0, ncol)
    own[:STRETCH, :] = dot(z[:STRETCH, :], wo[:, at]) + top_l[...].astype(F32)
    own[STRETCH:, :] = dot(z[STRETCH:, :], wo[:, at]) + low_r[...].astype(F32)


def mine_part(ids, z, wo, low_r, top_l):
    tok, nv = z.shape
    ncol = wo.shape[1] // RING
    return call(
        mine_body,
        [shape((tok, ncol))],
        (ids, z, wo, low_r, top_l),
        "mine_part",
        4 * tok * nv * ncol,
    )[0]


def add_body(ids, a1, b1, a2, b2, sent_r, sent_l, o1, o2):
    o1[:STRETCH, :] = (a1[...] + b1[:STRETCH, :].astype(F32)).astype(BF)
    o1[STRETCH:, :] = b1[STRETCH:, :]
    o2[...] = (a2[...] + b2[:STRETCH, :].astype(F32)).astype(BF)


def add_part(ids, a1, b1, a2, b2, sent_r, sent_l):
    return call(
        add_body,
        [shape(b1.shape, BF), shape(a2.shape, BF)],
        (ids, a1, b1, a2, b2, sent_r, sent_l),
        "add_part",
        2 * a1.size,
    )


def final_body(ids, own, top_r, low_l, mine, sq_r, sq_l, out):
    total = mine[0:1, :]
    for other in (sq_r, sq_l, top_r):
        more = other[STRETCH:, :512].astype(F32)
        total = total + (more[0:1, :] + more[1:2, :] + more[2:3, :])
    inv = lax.rsqrt(total * (1.0 / 5120.0) + 1e-05)
    inv = jnp.transpose(jnp.broadcast_to(inv, (128, inv.shape[1])))
    for block, got in ((0, top_r), (1, low_l)):
        rows = block_rows(block)
        scale = inv[rows, :]
        for low in range(0, out.shape[1], 128):
            c = slice(low, low + 128)
            out[rows, c] = ((own[rows, c] + got[:STRETCH, c].astype(F32)) * scale).astype(BF)


def final_part(ids, own, top_r, low_l, mine, sq_r, sq_l):
    return call(
        final_body,
        [shape(own.shape, BF)],
        (ids, own, top_r, low_l, mine, sq_r, sq_l),
        "final_part",
        4 * own.size,
    )[0]


def on_device(
    tokens,
    send_rows,
    send_counts,
    stretch_segments,
    main_proj,
    state_proj,
    step_proj,
    conv_main,
    conv_state,
    step_bias,
    decay_log,
    skip_gain,
    norm_gain,
    out_proj,
):
    ctx = lax.axis_index("ctx").astype(jnp.int32)
    head = lax.axis_index("head").astype(jnp.int32)
    tok, width = tokens.shape
    sources, slots = send_rows.shape[1:]
    heads = step_bias.shape[0]
    inner = main_proj.shape[2]
    head_dim = inner // heads

    send_list = send_rows.reshape(sources * slots)
    pick = (send_list[:, None] == jnp.arange(tok, dtype=jnp.int32)[None, :]).astype(BF)
    outgoing = dot(pick, tokens).astype(BF).reshape(sources, slots, width)
    arrived = lax.all_to_all(outgoing, "ctx", split_axis=0, concat_axis=0, tiled=True)

    blocks = tok // STRETCH
    block_ids = ctx * blocks + jnp.arange(blocks, dtype=jnp.int32)
    segment = jnp.take(stretch_segments, block_ids)
    before = jnp.take(stretch_segments, jnp.maximum(block_ids - 1, 0))
    carry = ((segment == before) & (block_ids > 0)).astype(jnp.int32)
    ring = jnp.stack([head, head + 3, head + 1, head + 2]) % RING
    ids = jnp.concatenate([ring, carry]).astype(jnp.int32)
    wm = flat_part(ids, main_proj)
    pad = ((0, 128 - heads),)
    head_rows = jnp.stack(
        [jnp.pad(step_bias, pad), jnp.pad(jnp.exp(decay_log), pad), jnp.pad(skip_gain, pad)]
    )
    head_rows = jnp.pad(head_rows, ((0, 5), (0, 0)))
    gain = norm_gain[None, :]

    column = jnp.take(send_counts, ctx, axis=1)
    begins = jnp.cumsum(column) - column
    slot = jnp.arange(slots, dtype=jnp.int32)[None, :]
    target = jnp.where(slot < column[:, None], begins[:, None] + slot, -1)
    target = target.reshape(1, sources * slots)
    arrived, wm, target, head_rows, gain, ids, step_proj = lax.optimization_barrier(
        (arrived, wm, target, head_rows, gain, ids, step_proj)
    )
    second, first, last = arrange_part(ids, target, arrived.reshape(sources * slots, width))
    weights = (state_proj, step_proj, wm)
    taps = (conv_state, conv_main, head_rows)

    r1 = turned(second, 1)
    l1 = turned(second, -1)
    t = shifted(last, 1)
    acc1 = own_part(ids, second, *weights)
    first = jnp.concatenate([t, first], axis=0)
    r1, l1, acc1, first = lax.optimization_barrier((r1, l1, acc1, first))
    cut = STRETCH // 2 + TAIL
    b1 = turned(r1[:cut], 1)
    b2 = turned(l1[cut:], -1)
    acc1 = next_part(ids, r1, l1, *weights, acc1)
    first, acc1 = lax.optimization_barrier((first, acc1))
    r0 = turned(first, 1)
    l0 = turned(first, -1)
    acc0 = own_part(ids, first, *weights)
    b1, b2, acc1, acc0 = lax.optimization_barrier((b1, b2, acc1, acc0))
    *block1, payload, mid, mid_step = second_part(ids, b1, b2, *weights, acc1, *taps)
    got_s = shifted(payload, 1)
    r0, l0, acc0, payload = lax.optimization_barrier((r0, l0, acc0, payload))
    cut = STRETCH // 2
    a1 = turned(r0[:cut], 1)
    a2 = turned(l0[cut:], -1)
    acc0 = next_part(ids, r0, l0, *weights, acc0)
    *block0, joined, joined_low, state0, end_row = first_part(
        ids, a1, a2, *weights, acc0, *taps, mid, mid_step, got_s
    )

    got_v = shifted(joined, 1)
    got_w = shifted(joined_low, 2)
    p, q = mix_part(ids, a1, a2, b1, b2, wm, acc0, acc1, head_rows, block0, block1)

    z, far_r, far_l, squares = gated_part(
        ids, p, q, block0[1], block1[1], got_s, got_v, got_w, state0, end_row, gain, out_proj
    )
    got_r = turned(far_r, 1)
    got_l = turned(far_l, -1)
    dir_r, dir_l, top_r, low_l = near_part(ids, z, out_proj, far_r, far_l)
    low_r = turned(dir_r, 1)
    top_l = turned(dir_l, -1)
    sum_r, sum_l = add_part(ids, top_r, got_r, low_l, got_l, dir_r, dir_l)
    top_r = turned(sum_r, 1)
    low_l = turned(sum_l, -1)
    own = mine_part(ids, z, out_proj, low_r, top_l)
    return final_part(ids, own, top_r, low_l, squares, got_r, got_l)


def solution(mesh):
    return jax.shard_map(
        on_device,
        mesh=mesh,
        in_specs=(
            P("ctx", "head"),
            P("ctx", None, None),
            P(),
            P(),
            P(None, None, "head"),
            P(),
            P(None, "head"),
            P(None, "head"),
            P(),
            P("head"),
            P("head"),
            P("head"),
            P("head"),
            P("head", None),
        ),
        out_specs=P("ctx", "head"),
        check_vma=False,
    )
```
